128 devices in a mesh: seq: 32 (over z, y, x_lo), dp: 4 (over x_hi, core).
Axes of the slice: x: 4 (x_hi: 2, x_lo: 2; x = x_hi * 2 + x_lo), y: 4, z: 4, core: 2. Of those that a mesh axis runs over, the one named last changes fastest.
Arguments:
- clips: bfloat16 [4, 32, 256, 1152], P('dp', 'seq'), may hold values from -6 to 6
- cotangent: bfloat16 [4, 32, 256, 1152], P('dp', 'seq'), may hold values from -6 to 6
- w_qkv_space: bfloat16 [1152, 1728], replicated, may hold values from -0.1875 to 0.1875
- w_out_space: bfloat16 [1152, 576], replicated, may hold values from -0.25 to 0.25
- w_qkv_time: bfloat16 [1152, 1728], replicated, may hold values from -0.1875 to 0.1875
- w_out_time: bfloat16 [1152, 576], replicated, may hold values from -0.25 to 0.25
Outputs:
- mixed: bfloat16 [4, 32, 256, 1152], P('dp', 'seq')
- grad_clips: bfloat16 [4, 32, 256, 1152], P('dp', 'seq')
- grad_qkv_space: float32 [1152, 1728], P(('seq', 'dp'))
- grad_out_space: float32 [1152, 576], P(('seq', 'dp'))
- grad_qkv_time: float32 [1152, 1728], P(('seq', 'dp'))
- grad_out_time: float32 [1152, 576], P(('seq', 'dp'))
The draws below stay inside these ranges and needn't reach their ends.
All inputs are finite; a program needn't handle non-finite values.
Results may differ from the reference program's by a relative error of at most 0.022.
Values may be sent and summed in bfloat16 or wider, within the bound.
No kernel may reach another device: no remote copies, remote signals or barrier semaphores. Data moves between devices by JAX's collectives and lax.ppermute only.
A program may use at most 128 MiB of HBM per device.

```python
import jax
import jax.numpy as jnp
from jax import lax

D = 1152
HEADS = 8
HEAD_DIM = 72
P_SIZE = 256
HK = 576
FRAMES = 32
CLIPS = 4
TOKENS = 32768


def raised(values, key, source, target, shards_of, factor):
    def block_of(position):
        return (jnp.arange(values.shape[position]) // (values.shape[position] // shards_of)).reshape((-1,) + (1,) * (values.ndim - 1 - position))

    near = jax.random.permutation(key, shards_of)[block_of(target)]
    far = (block_of(target) + shards_of // 2) % shards_of
    return jnp.where((block_of(source) == near) | (block_of(source) == far), factor * values, values)


def steps_of(rng, extent, pieces, least, top_value):
    gain, own = 1.0, jax.random.fold_in(rng, 6)
    for dim, blocks in pieces:
        heights = jnp.exp(jax.random.uniform(jax.random.fold_in(own, dim), (blocks,), jnp.float32, least / len(pieces), top_value / len(pieces)))
        gain = gain * jnp.repeat(heights, extent[dim] // blocks).reshape([-1 if axis == dim else 1 for axis in range(len(extent))])
    return gain


def normal_values(rng, extent, deviation, reach, pieces=(), held_as=jnp.bfloat16):
    array = jax.random.normal(rng, extent, jnp.float32) * deviation
    if len(pieces) > 0:
        array = steps_of(rng, extent, pieces, -0.22, 0.18) * array
    return jnp.clip(array, min=-reach, max=reach).astype(held_as)


def bell_draw_with(rng, extent, scale, limit, cuts, heavy, dtype=jnp.bfloat16):
    entries = scale * jax.random.normal(rng, extent, jnp.float32)
    if cuts:
        entries = entries * steps_of(rng, extent, cuts, -0.22, 0.18)
    return jnp.clip(raised(entries, jax.random.fold_in(rng, 3), *heavy), -limit, limit).astype(dtype)


def setup_inputs(seed: int = 0) -> dict:
    splits = jax.random.split(jax.random.key(seed), 7)
    clips = normal_values(splits[0], (CLIPS, FRAMES, P_SIZE, D), 1.0, 6.0, ((0, 4), (1, 32)))
    cotangent = bell_draw_with(splits[1], (CLIPS, FRAMES, P_SIZE, D), 1.0, 6.0, ((0, 4), (1, 32)), (1, 3, 32, 2.75))
    w_qkv_space = normal_values(splits[2], (D, 3 * HK), D ** -0.5, 0.1875)
    w_out_space = normal_values(splits[3], (D, HK), HK ** -0.5, 0.25)
    w_qkv_time = normal_values(splits[4], (D, 3 * HK), D ** -0.5, 0.1875)
    w_out_time = normal_values(splits[5], (D, HK), HK ** -0.5, 0.25)
    return dict(clips=clips, cotangent=cotangent, w_qkv_space=w_qkv_space, w_out_space=w_out_space, w_qkv_time=w_qkv_time, w_out_time=w_out_time)


EPS = 1e-06

def layer_norm(tokens):
    values = tokens.astype(jnp.float32)
    center = values - lax.optimization_barrier(jnp.mean(values, axis=-1, keepdims=True))
    spread = lax.optimization_barrier(jnp.mean(center * center, axis=-1, keepdims=True))
    return (center * lax.rsqrt(spread + EPS)).astype(jnp.bfloat16)

def attend(packed, temporal):
    first, second = (packed.shape[0], packed.shape[1])
    parts = packed.reshape(first, second, 3, HEADS, HEAD_DIM)
    query, keys, values = (parts[:, :, 0], parts[:, :, 1], parts[:, :, 2])
    if temporal:
        form_scores, form_mix = ('qbhd,kbhd->bhqk', 'bhqk,kbhd->qbhd')
    else:
        form_scores, form_mix = ('aqhd,akhd->ahqk', 'ahqk,akhd->aqhd')
    scores = jnp.einsum(form_scores, query, keys, preferred_element_type=jnp.float32) * HEAD_DIM ** (-0.5)
    peak = lax.optimization_barrier(jnp.max(scores, axis=-1, keepdims=True))
    weights = jnp.exp(scores - peak)
    weights = (weights / lax.optimization_barrier(jnp.sum(weights, axis=-1, keepdims=True))).astype(jnp.bfloat16)
    mixout = jnp.einsum(form_mix, weights, values, preferred_element_type=jnp.float32)
    return mixout.astype(jnp.bfloat16).reshape(first, second, HEADS * HEAD_DIM)

def project_back(left, weight):
    return lax.dot_general(left, weight, (((1,), (1,)), ((), ())), preferred_element_type=jnp.float32)

def outer_sum(left, right):
    return lax.dot_general(left, right, (((0,), (0,)), ((), ())), preferred_element_type=jnp.float32)

def clip_step(clip, cot, w_qkv_space, w_out_space, w_qkv_time, w_out_time):
    frames, patches, width = clip.shape
    count = frames * patches
    flat = clip.reshape(count, width)
    normed_space, norm_space_back = jax.vjp(layer_norm, flat)
    qkv_space = jnp.dot(normed_space, w_qkv_space, preferred_element_type=jnp.float32).astype(jnp.bfloat16)
    attn_space, attn_space_back = jax.vjp(lambda t: attend(t.reshape(frames, patches, -1), False).reshape(count, -1), qkv_space)
    hidden = (flat.astype(jnp.float32) + project_back(attn_space, w_out_space)).astype(jnp.bfloat16)
    normed_time, norm_time_back = jax.vjp(layer_norm, hidden)
    qkv_time = jnp.dot(normed_time, w_qkv_time, preferred_element_type=jnp.float32).astype(jnp.bfloat16)
    attn_time, attn_time_back = jax.vjp(lambda t: attend(t.reshape(frames, patches, -1), True).reshape(count, -1), qkv_time)
    mixed = (hidden.astype(jnp.float32) + project_back(attn_time, w_out_time)).astype(jnp.bfloat16)
    grad_top = cot.reshape(count, width)
    dattn_time = jnp.dot(grad_top, w_out_time, preferred_element_type=jnp.float32).astype(jnp.bfloat16)
    dqkv_time = attn_time_back(dattn_time)[0]
    dnormed_time = project_back(dqkv_time, w_qkv_time).astype(jnp.bfloat16)
    dres_time = norm_time_back(dnormed_time)[0]
    dhidden = grad_top + dres_time
    dattn_space = jnp.dot(dhidden, w_out_space, preferred_element_type=jnp.float32).astype(jnp.bfloat16)
    dqkv_space = attn_space_back(dattn_space)[0]
    dnormed_space = project_back(dqkv_space, w_qkv_space).astype(jnp.bfloat16)
    dres_space = norm_space_back(dnormed_space)[0]
    grad_clip = dhidden + dres_space
    scale = jnp.float32(TOKENS ** (-0.5))
    terms = (outer_sum(normed_space, dqkv_space) * scale, outer_sum(dhidden, attn_space) * scale, outer_sum(normed_time, dqkv_time) * scale, outer_sum(grad_top, attn_time) * scale)
    return (mixed.reshape(clip.shape), grad_clip.reshape(clip.shape), terms)

def reference(clips, cotangent, w_qkv_space, w_out_space, w_qkv_time, w_out_time):

    def per_clip(pair):
        return clip_step(pair[0], pair[1], w_qkv_space, w_out_space, w_qkv_time, w_out_time)
    mixed, grad_clips, terms = lax.map(per_clip, (clips, cotangent))
    sums = [lax.optimization_barrier(jnp.sum(term, axis=0)) for term in terms]
    return (mixed, grad_clips, sums[0], sums[1], sums[2], sums[3])
```

```python
import functools
import math

import jax
import jax.numpy as jnp
import numpy as np
from jax import lax
from jax.experimental import pallas as pl
from jax.experimental.pallas import tpu as pltpu
from jax.sharding import Mesh
from jax.sharding import PartitionSpec as P

HEADS = 8
HEAD_DIM = 72
HK = HEADS * HEAD_DIM
EPS = 1e-06
LANES = 128
F32 = jnp.float32
BF16 = jnp.bfloat16


def windows():
    out = []
    for head in range(HEADS):
        low, high = head * HEAD_DIM, (head + 1) * HEAD_DIM
        start = low // LANES * LANES
        stop = min(-(-high // LANES) * LANES, HK)
        out.append((low, high, start, stop))
    return out


def dot_nn(a, b):
    return lax.dot_general(a, b, (((1,), (0,)), ((), ())), preferred_element_type=F32)


def dot_nt(a, b):
    return lax.dot_general(a, b, (((1,), (1,)), ((), ())), preferred_element_type=F32)


def dot_tn(a, b):
    return lax.dot_general(a, b, (((0,), (0,)), ((), ())), preferred_element_type=F32)


def norm_parts(tokens):
    center = tokens - jnp.mean(tokens, axis=-1, keepdims=True)
    spread = jnp.mean(center * center, axis=-1, keepdims=True)
    rate = lax.rsqrt(spread + EPS)
    return center * rate, rate


def norm_back(grad, normed, rate):
    first = jnp.mean(grad, axis=-1, keepdims=True)
    second = jnp.mean(grad * normed, axis=-1, keepdims=True)
    return rate * (grad - first - normed * second)


def split_qkv(qkv):
    return qkv[:, :HK], qkv[:, HK : 2 * HK], qkv[:, 2 * HK :]


class HeadSum:
    def __init__(self):
        self.slabs = [None] * -(-HK // LANES)

    def put(self, head, piece):
        low, high, start, stop = windows()[head]
        for slab in range(start // LANES, -(-stop // LANES)):
            left, right = slab * LANES, min((slab + 1) * LANES, HK)
            part = piece[:, left - start : right - start]
            held = self.slabs[slab]
            if held is not None:
                lane = left + lax.broadcasted_iota(jnp.int32, part.shape, 1)
                part = jnp.where((lane >= low) & (lane < high), part, held)
            self.slabs[slab] = part

    def whole(self, dtype):
        return jnp.concatenate([slab.astype(dtype) for slab in self.slabs], axis=1)


def head_part(array, head):
    low, high, start, stop = windows()[head]
    part = array[:, start:stop]
    lane = start + lax.broadcasted_iota(jnp.int32, part.shape, 1)
    return jnp.where((lane >= low) & (lane < high), part, jnp.zeros_like(part))


def head_window(array, head):
    _, _, start, stop = windows()[head]
    return array[:, start:stop]


def probs_t(query, keys, head, keep):
    scores = dot_nt(head_part(keys, head), head_window(query, head)) * HEAD_DIM ** (-0.5)
    if keep is not None:
        scores = jnp.where(keep, scores, -1e30)
    peak = jnp.max(scores, axis=0, keepdims=True)
    weights = jnp.exp(scores - peak)
    return weights / jnp.sum(weights, axis=0, keepdims=True)


def same_patch(count, patches):
    row = lax.broadcasted_iota(jnp.int32, (count, count), 0)
    col = lax.broadcasted_iota(jnp.int32, (count, count), 1)
    return lax.rem(row, patches) == lax.rem(col, patches)


def space_forward(x_ref, cot_ref, w_qkv_ref, w_out_ref, w_time_ref, send_ref, qkv_ref, attn_ref, normed_ref):
    x = x_ref[...].astype(F32)
    normed = norm_parts(x)[0].astype(BF16)
    normed_ref[...] = normed
    qkv = dot_nn(normed, w_qkv_ref[...]).astype(BF16)
    qkv_ref[...] = qkv
    query, keys, values = split_qkv(qkv)
    mix = HeadSum()
    for head in range(HEADS):
        weights = probs_t(query, keys, head, None).astype(BF16)
        mix.put(head, dot_tn(weights, head_window(values, head)))
    attn = mix.whole(BF16)
    attn_ref[...] = attn
    width = x.shape[1]
    send_ref[:, :width] = (x + dot_nt(attn, w_out_ref[...])).astype(BF16)
    send_ref[:, width:] = dot_nn(cot_ref[...], w_time_ref[...]).astype(BF16)


def attention_back(query, keys, values, dmix, keep, forward):
    mix, dq, dk, dv = HeadSum(), HeadSum(), HeadSum(), HeadSum()
    for head in range(HEADS):
        weights = probs_t(query, keys, head, keep)
        rounded = weights.astype(BF16)
        if forward:
            mix.put(head, dot_tn(rounded, head_window(values, head)))
        dprobs = dot_nt(head_part(values, head), head_window(dmix, head)).astype(BF16).astype(F32)
        total = jnp.sum(weights * dprobs, axis=0, keepdims=True)
        dscores = (weights * (dprobs - total) * HEAD_DIM ** (-0.5)).astype(BF16)
        dv.put(head, dot_nn(rounded, head_window(dmix, head)))
        dk.put(head, dot_nn(dscores, head_window(query, head)))
        dq.put(head, dot_tn(dscores, head_window(keys, head)))
    dqkv = jnp.concatenate([dq.whole(BF16), dk.whole(BF16), dv.whole(BF16)], axis=1)
    return (mix.whole(BF16) if forward else None), dqkv


def time_both(patches, recv_ref, w_qkv_ref, back_ref, normed_ref, dqkv_ref):
    width = w_qkv_ref.shape[0]
    hidden = recv_ref[:, :width].astype(F32)
    normed, rate = norm_parts(hidden)
    rounded = normed.astype(BF16)
    normed_ref[...] = rounded
    qkv = dot_nn(rounded, w_qkv_ref[...]).astype(BF16)
    query, keys, values = split_qkv(qkv)
    keep = same_patch(hidden.shape[0], patches)
    attn, dqkv = attention_back(query, keys, values, recv_ref[:, width:], keep, True)
    dqkv_ref[...] = dqkv
    back_ref[:, width:] = attn
    dnormed = dot_nt(dqkv, w_qkv_ref[...]).astype(BF16).astype(F32)
    back_ref[:, :width] = norm_back(dnormed, normed, rate).astype(BF16)


def space_backward(
    core_ref, cot_ref, recv_ref, qkv_ref, attn_ref, w_out_ref, dhidden_ref, dqkv_ref, keep_ref, send_ref
):
    width = cot_ref.shape[1]
    dhidden = cot_ref[...] + recv_ref[:, :width]
    dhidden_ref[...] = dhidden
    dattn = dot_nn(dhidden, w_out_ref[...]).astype(BF16)
    query, keys, values = split_qkv(qkv_ref[...])
    dqkv = attention_back(query, keys, values, dattn, None, False)[1]
    dqkv_ref[...] = dqkv
    pair_up(core_ref[0], dqkv, attn_ref[...], keep_ref, send_ref)


def space_finish(x_ref, dhidden_ref, dqkv_ref, w_qkv_ref, grad_ref):
    normed, rate = norm_parts(x_ref[...].astype(F32))
    dnormed = dot_nt(dqkv_ref[...], w_qkv_ref[...]).astype(BF16).astype(F32)
    dres = norm_back(dnormed, normed, rate).astype(BF16)
    grad_ref[...] = dhidden_ref[...] + dres


def call(kernel, outs, *args, flops=0):
    size = sum(a.size * a.dtype.itemsize for a in args) + sum(math.prod(shape) * 2 for shape, _ in outs)
    shapes = [jax.ShapeDtypeStruct(shape, dtype) for shape, dtype in outs]
    return pl.pallas_call(
        kernel,
        out_shape=shapes,
        in_specs=[
            pl.BlockSpec(memory_space=pltpu.SMEM if a.dtype == jnp.int32 else pltpu.VMEM) for a in args
        ],
        out_specs=[pl.BlockSpec(memory_space=pltpu.VMEM)] * len(outs),
        compiler_params=pltpu.CompilerParams(vmem_limit_bytes=40 * 1024 * 1024),
        cost_estimate=pl.CostEstimate(flops=flops, bytes_accessed=size, transcendentals=0),
    )(*args)


def permutation(width, chips):
    rows = width // chips
    table = np.zeros((3, chips, 8, width), np.float32)
    for chip in range(chips):
        for lane in range(8):
            table[0, chip, lane, chip * rows + lane] = 1
            table[1, chip, lane, chip * rows + 8 + lane] = 1
        for lane in range(6):
            table[2, chip, lane, chip * rows + 16 + lane % 2] = 1
    return table.reshape(3 * chips * 8, width).astype(jnp.bfloat16)


def transpose_rows(perm_ref, tokens_ref, out_ref):
    out_ref[...] = dot_nt(perm_ref[...], tokens_ref[...]).astype(BF16)


def mix_out(send_ref, recv_ref, w_out_ref, mixed_ref):
    width = w_out_ref.shape[0]
    mixed = send_ref[:, :width].astype(F32) + dot_nt(recv_ref[:, width:], w_out_ref[...])
    mixed_ref[...] = mixed.astype(BF16)


def pair_up(core, dqkv, attn, keep_ref, send_ref):
    second = jnp.concatenate([dqkv[:, 2 * HK :], attn], axis=1)
    first = dqkv[:, : 2 * HK]
    keep_ref[...] = jnp.where(core == 0, first, second)
    send_ref[...] = jnp.where(core == 0, second, first)


def time_pair(core_ref, dqkv_ref, recv_ref, keep_ref, send_ref):
    pair_up(core_ref[0], dqkv_ref[...], recv_ref[:, recv_ref.shape[1] - HK :], keep_ref, send_ref)


def weight_terms(core_ref, in_own, in_got, out_own, out_got, own_ref, got_ref, chunk_ref):
    block = in_own.shape[0] // 3
    low, high = HK // LANES * LANES, -(-HK // LANES) * LANES
    width = own_ref.shape[1]
    third = width // 3

    def fill(second_own, second_got):
        for part in range(3):
            rows = pl.ds(part * block, block)
            left = dot_nn(in_own[rows, :], own_ref[:, :high]) + dot_nn(in_got[rows, :], got_ref[:, :high])
            right = dot_nn(second_own[rows, :], own_ref[:, low:]) + dot_nn(
                second_got[rows, :], got_ref[:, low:]
            )
            lane = low + lax.broadcasted_iota(jnp.int32, (block, high - low), 1)
            middle = jnp.where(lane < HK, left[:, low:], right[:, : high - low])
            whole = jnp.concatenate([left[:, :low], middle, right[:, high - low :]], axis=1)
            if part < 2:
                chunk_ref[:, part * width : (part + 1) * width] = whole.astype(BF16)
            else:
                row = lax.rem(lax.broadcasted_iota(jnp.int32, (block, third), 0), 8)
                rest = jnp.where(
                    row < 2,
                    whole[:, :third],
                    jnp.where(row < 4, whole[:, third : 2 * third], whole[:, 2 * third :]),
                )
                chunk_ref[:, 2 * width :] = rest.astype(BF16)

    @pl.when(core_ref[0] == 0)
    def _():
        fill(in_own, in_got)

    @pl.when(core_ref[0] != 0)
    def _():
        fill(out_own, out_got)


def add_chunks(scale, core_ref, chunk_ref, keep_ref, send_ref):
    count, lanes = chunk_ref.shape
    total = chunk_ref[:16, :].astype(F32)
    for start in range(16, count, 16):
        total = total + chunk_ref[start : start + 16, :].astype(F32)
    total = (total[:8] + total[8:]) * scale
    width = keep_ref.shape[1]
    third = width // 3
    first, second, rest = total[:, :width], total[:, width : 2 * width], total[:, 2 * width :]
    last = jnp.concatenate([rest[0:2], rest[2:4], rest[4:6]], axis=1)
    low = jnp.concatenate([first, second[:1]], axis=0)
    high = jnp.concatenate([second[1:], last], axis=0)
    core = core_ref[0]
    keep_ref[...] = jnp.where(core == 0, low, high)
    send_ref[...] = jnp.where(core == 0, high, low)


def place_rows(core_ref, keep_ref, got_ref, qkv_ref, out_ref):
    core = core_ref[0]
    keep, got = keep_ref[...], got_ref[...]
    first = jnp.where(core == 0, keep, got)
    second = jnp.where(core == 0, got, keep)
    qkv_ref[:, : 2 * HK] = first
    qkv_ref[:, 2 * HK :] = second[:, :HK]
    out_ref[...] = second[:, HK:]


SEQ = ("z", "y", "xl")
CHIPS = ("z", "y", "xl", "xh")


def on_device(clips, cotangent, w_qkv_space, w_out_space, w_qkv_time, w_out_time):
    patches, width = clips.shape[2], clips.shape[3]
    frames = lax.axis_size(SEQ)
    chips = lax.axis_size(CHIPS)
    own_patches = patches // frames
    count = patches
    qkv_cols = w_qkv_space.shape[1]
    scale = 1.0 / math.sqrt(count * frames * lax.axis_size(("xh", "c")))
    core = lax.axis_index("c").astype(jnp.int32).reshape(1)
    x = clips.reshape(count, width)
    top = cotangent.reshape(count, width)
    perm = jnp.asarray(permutation(width, chips))
    pairs = [(0, 1), (1, 0)]

    def swap(array):
        return lax.ppermute(array, "c", pairs)

    def exchange(array, axes, parts):
        lanes = array.shape[1]
        array = lax.all_to_all(
            array.reshape(parts, -1, lanes), axes, split_axis=0, concat_axis=0, tiled=True
        )
        return array.reshape(-1, lanes)

    def rows_of(tokens):
        out = call(transpose_rows, [((perm.shape[0], count), BF16)], perm, tokens, flops=10**9)[0]
        return out, swap(out)

    send, qkv_space, attn_space, normed_space = call(
        space_forward,
        [((count, width + HK), BF16), ((count, qkv_cols), BF16), ((count, HK), BF16), ((count, width), BF16)],
        x, top, w_qkv_space, w_out_space, w_out_time, flops=3 * 10**9,
    )
    recv = exchange(send, SEQ, frames)
    back, normed_time, dqkv_time = call(
        functools.partial(time_both, own_patches),
        [((count, width + HK), BF16), ((count, width), BF16), ((count, qkv_cols), BF16)],
        recv, w_qkv_time, flops=5 * 10**9,
    )
    recv = exchange(back, SEQ, frames)
    rows_norm_space = rows_of(normed_space)
    rows_top = rows_of(top)
    rows_norm_time = rows_of(normed_time)
    half = ((count, width), BF16)
    keep, give = call(time_pair, [half, half], core, dqkv_time, recv)
    chunk_shape = ((8 * chips, 2 * width + width // 3), BF16)
    terms_time = call(
        weight_terms, [chunk_shape], core, *rows_norm_time, *rows_top, keep, swap(give),
        flops=2 * 10**9,
    )[0]
    got_time = exchange(terms_time, CHIPS, chips)
    dhidden, dqkv_space, keep, give = call(
        space_backward, [half, ((count, qkv_cols), BF16), half, half],
        core, top, recv, qkv_space, attn_space, w_out_space, flops=3 * 10**9,
    )
    rows_dhidden = rows_of(dhidden)
    terms_space = call(
        weight_terms, [chunk_shape], core, *rows_norm_space, *rows_dhidden, keep, swap(give), flops=2 * 10**9
    )[0]
    got_space = exchange(terms_space, CHIPS, chips)
    grad_clips = call(
        space_finish, [half], x, dhidden, dqkv_space, w_qkv_space, flops=10**9
    )[0]
    mixed = call(mix_out, [half], send, recv, w_out_time, flops=10**9)[0]

    def finish(got):
        rows = width // chips // 2
        own, other = call(
            functools.partial(add_chunks, scale), [((rows, width), F32), ((rows, width), F32)], core, got
        )
        return call(
            place_rows, [((rows, qkv_cols), F32), ((rows, HK), F32)], core, own, swap(other)
        )

    grad_qkv_time, grad_out_time = finish(got_time)
    grad_qkv_space, grad_out_space = finish(got_space)
    return (
        mixed.reshape(clips.shape),
        grad_clips.reshape(clips.shape),
        grad_qkv_space,
        grad_out_space,
        grad_qkv_time,
        grad_out_time,
    )


def solution(mesh):
    fine = Mesh(mesh.devices.reshape(4, 4, 2, 2, 2), ("z", "y", "xl", "xh", "c"))
    tokens = P(("xh", "c"), SEQ, None, None)
    rows = P(("z", "y", "xl", "xh", "c"), None)
    return jax.shard_map(
        on_device,
        mesh=fine,
        in_specs=(tokens, tokens, P(), P(), P(), P()),
        out_specs=(tokens, tokens, rows, rows, rows, rows),
        check_vma=False,
    )
```

```python
import functools
import math

import jax
import jax.numpy as jnp
import numpy as np
from jax import lax
from jax.experimental import pallas as pl
from jax.experimental.pallas import tpu as pltpu
from jax.sharding import Mesh
from jax.sharding import PartitionSpec as P

HEADS = 8
HEAD_DIM = 72
HK = HEADS * HEAD_DIM
EPS = 1e-06
LANES = 128
F32 = jnp.float32
BF16 = jnp.bfloat16


def windows():
    out = []
    for head in range(HEADS):
        low, high = head * HEAD_DIM, (head + 1) * HEAD_DIM
        start = low // LANES * LANES
        stop = min(-(-high // LANES) * LANES, HK)
        out.append((low, high, start, stop))
    return out


def dot_nn(a, b):
    return lax.dot_general(a, b, (((1,), (0,)), ((), ())), preferred_element_type=F32)


def dot_nt(a, b):
    return lax.dot_general(a, b, (((1,), (1,)), ((), ())), preferred_element_type=F32)


def dot_tn(a, b):
    return lax.dot_general(a, b, (((0,), (0,)), ((), ())), preferred_element_type=F32)


def norm_parts(tokens):
    center = tokens - jnp.mean(tokens, axis=-1, keepdims=True)
    spread = jnp.mean(center * center, axis=-1, keepdims=True)
    rate = lax.rsqrt(spread + EPS)
    return center * rate, rate


def norm_back(grad, normed, rate):
    first = jnp.mean(grad, axis=-1, keepdims=True)
    second = jnp.mean(grad * normed, axis=-1, keepdims=True)
    return rate * (grad - first - normed * second)


def split_qkv(qkv):
    return qkv[:, :HK], qkv[:, HK : 2 * HK], qkv[:, 2 * HK :]


class HeadSum:
    def __init__(self):
        self.slabs = [None] * -(-HK // LANES)

    def put(self, head, piece):
        low, high, start, stop = windows()[head]
        for slab in range(start // LANES, -(-stop // LANES)):
            left, right = slab * LANES, min((slab + 1) * LANES, HK)
            part = piece[:, left - start : right - start]
            held = self.slabs[slab]
            if held is not None:
                lane = left + lax.broadcasted_iota(jnp.int32, part.shape, 1)
                part = jnp.where((lane >= low) & (lane < high), part, held)
            self.slabs[slab] = part

    def whole(self, dtype):
        return jnp.concatenate([slab.astype(dtype) for slab in self.slabs], axis=1)


def head_part(array, head):
    low, high, start, stop = windows()[head]
    part = array[:, start:stop]
    lane = start + lax.broadcasted_iota(jnp.int32, part.shape, 1)
    return jnp.where((lane >= low) & (lane < high), part, jnp.zeros_like(part))


def head_window(array, head):
    _, _, start, stop = windows()[head]
    return array[:, start:stop]


def probs_t(query, keys, head, keep):
    scores = dot_nt(head_part(keys, head), head_window(query, head)) * HEAD_DIM ** (-0.5)
    if keep is not None:
        scores = jnp.where(keep, scores, -1e30)
    peak = jnp.max(scores, axis=0, keepdims=True)
    weights = jnp.exp(scores - peak)
    return weights / jnp.sum(weights, axis=0, keepdims=True)


def same_patch(count, patches):
    row = lax.broadcasted_iota(jnp.int32, (count, count), 0)
    col = lax.broadcasted_iota(jnp.int32, (count, count), 1)
    return lax.rem(row, patches) == lax.rem(col, patches)


def space_forward(x_ref, cot_ref, w_qkv_ref, w_out_ref, w_time_ref, send_ref, qkv_ref, attn_ref, normed_ref):
    x = x_ref[...].astype(F32)
    normed = norm_parts(x)[0].astype(BF16)
    normed_ref[...] = normed
    qkv = dot_nt(normed, w_qkv_ref[...]).astype(BF16)
    qkv_ref[...] = qkv
    query, keys, values = split_qkv(qkv)
    mix = HeadSum()
    for head in range(HEADS):
        weights = probs_t(query, keys, head, None).astype(BF16)
        mix.put(head, dot_tn(weights, head_window(values, head)))
    attn = mix.whole(BF16)
    attn_ref[...] = attn
    width = x.shape[1]
    send_ref[:, :width] = (x + dot_nn(attn, w_out_ref[...])).astype(BF16)
    send_ref[:, width:] = dot_nt(cot_ref[...], w_time_ref[...]).astype(BF16)


def attention_back(query, keys, values, dmix, keep, forward):
    mix, dq, dk, dv = HeadSum(), HeadSum(), HeadSum(), HeadSum()
    for head in range(HEADS):
        weights = probs_t(query, keys, head, keep)
        rounded = weights.astype(BF16)
        if forward:
            mix.put(head, dot_tn(rounded, head_window(values, head)))
        dprobs = dot_nt(head_part(values, head), head_window(dmix, head)).astype(BF16).astype(F32)
        total = jnp.sum(weights * dprobs, axis=0, keepdims=True)
        dscores = (weights * (dprobs - total) * HEAD_DIM ** (-0.5)).astype(BF16)
        dv.put(head, dot_nn(rounded, head_window(dmix, head)))
        dk.put(head, dot_nn(dscores, head_window(query, head)))
        dq.put(head, dot_tn(dscores, head_window(keys, head)))
    dqkv = jnp.concatenate([dq.whole(BF16), dk.whole(BF16), dv.whole(BF16)], axis=1)
    return (mix.whole(BF16) if forward else None), dqkv


def time_both(patches, recv_ref, w_qkv_ref, back_ref, normed_ref, dqkv_ref):
    width = w_qkv_ref.shape[1]
    hidden = recv_ref[:, :width].astype(F32)
    normed, rate = norm_parts(hidden)
    rounded = normed.astype(BF16)
    normed_ref[...] = rounded
    qkv = dot_nt(rounded, w_qkv_ref[...]).astype(BF16)
    query, keys, values = split_qkv(qkv)
    keep = same_patch(hidden.shape[0], patches)
    attn, dqkv = attention_back(query, keys, values, recv_ref[:, width:], keep, True)
    dqkv_ref[...] = dqkv
    back_ref[:, width:] = attn
    dnormed = dot_nn(dqkv, w_qkv_ref[...]).astype(BF16).astype(F32)
    back_ref[:, :width] = norm_back(dnormed, normed, rate).astype(BF16)


def space_backward(
    core_ref, cot_ref, recv_ref, qkv_ref, attn_ref, w_out_ref, dhidden_ref, dqkv_ref, keep_ref, send_ref
):
    width = cot_ref.shape[1]
    dhidden = cot_ref[...] + recv_ref[:, :width]
    dhidden_ref[...] = dhidden
    dattn = dot_nt(dhidden, w_out_ref[...]).astype(BF16)
    query, keys, values = split_qkv(qkv_ref[...])
    dqkv = attention_back(query, keys, values, dattn, None, False)[1]
    dqkv_ref[...] = dqkv
    pair_up(core_ref[0], dqkv, attn_ref[...], keep_ref, send_ref)


def space_finish(x_ref, dhidden_ref, dqkv_ref, w_qkv_ref, grad_ref):
    normed, rate = norm_parts(x_ref[...].astype(F32))
    dnormed = dot_nn(dqkv_ref[...], w_qkv_ref[...]).astype(BF16).astype(F32)
    dres = norm_back(dnormed, normed, rate).astype(BF16)
    grad_ref[...] = dhidden_ref[...] + dres


def call(kernel, outs, *args, flops=0):
    size = sum(a.size * a.dtype.itemsize for a in args) + sum(math.prod(shape) * 2 for shape, _ in outs)
    shapes = [jax.ShapeDtypeStruct(shape, dtype) for shape, dtype in outs]
    return pl.pallas_call(
        kernel,
        out_shape=shapes,
        in_specs=[
            pl.BlockSpec(memory_space=pltpu.SMEM if a.dtype == jnp.int32 else pltpu.VMEM) for a in args
        ],
        out_specs=[pl.BlockSpec(memory_space=pltpu.VMEM)] * len(outs),
        compiler_params=pltpu.CompilerParams(vmem_limit_bytes=8 * 1024 * 1024),
        cost_estimate=pl.CostEstimate(flops=flops, bytes_accessed=size, transcendentals=0),
    )(*args)


def permutation(width, chips):
    rows = width // chips
    table = np.zeros((3, chips, 8, width), np.float32)
    for chip in range(chips):
        for lane in range(8):
            table[0, chip, lane, chip * rows + lane] = 1
            table[1, chip, lane, chip * rows + 8 + lane] = 1
        for lane in range(6):
            table[2, chip, lane, chip * rows + 16 + lane % 2] = 1
    return table.reshape(3 * chips * 8, width).astype(jnp.bfloat16)


def transpose_rows(perm_ref, tokens_ref, out_ref):
    out_ref[...] = dot_nt(perm_ref[...], tokens_ref[...]).astype(BF16)


def mix_out(send_ref, recv_ref, w_out_ref, mixed_ref):
    width = w_out_ref.shape[1]
    mixed = send_ref[:, :width].astype(F32) + dot_nn(recv_ref[:, width:], w_out_ref[...])
    mixed_ref[...] = mixed.astype(BF16)


def pair_up(core, dqkv, attn, keep_ref, send_ref):
    second = jnp.concatenate([dqkv[:, 2 * HK :], attn], axis=1)
    first = dqkv[:, : 2 * HK]
    keep_ref[...] = jnp.where(core == 0, first, second)
    send_ref[...] = jnp.where(core == 0, second, first)


def time_pair(core_ref, dqkv_ref, recv_ref, keep_ref, send_ref):
    pair_up(core_ref[0], dqkv_ref[...], recv_ref[:, recv_ref.shape[1] - HK :], keep_ref, send_ref)


def weight_terms(core_ref, in_own, in_got, out_own, out_got, own_ref, got_ref, chunk_ref):
    block = in_own.shape[0] // 3
    low, high = HK // LANES * LANES, -(-HK // LANES) * LANES
    width = own_ref.shape[1]
    third = width // 3

    def fill(second_own, second_got):
        for part in range(3):
            rows = pl.ds(part * block, block)
            left = dot_nn(in_own[rows, :], own_ref[:, :high]) + dot_nn(in_got[rows, :], got_ref[:, :high])
            right = dot_nn(second_own[rows, :], own_ref[:, low:]) + dot_nn(
                second_got[rows, :], got_ref[:, low:]
            )
            lane = low + lax.broadcasted_iota(jnp.int32, (block, high - low), 1)
            middle = jnp.where(lane < HK, left[:, low:], right[:, : high - low])
            whole = jnp.concatenate([left[:, :low], middle, right[:, high - low :]], axis=1)
            if part < 2:
                chunk_ref[:, part * width : (part + 1) * width] = whole.astype(BF16)
            else:
                row = lax.rem(lax.broadcasted_iota(jnp.int32, (block, third), 0), 8)
                rest = jnp.where(
                    row < 2,
                    whole[:, :third],
                    jnp.where(row < 4, whole[:, third : 2 * third], whole[:, 2 * third :]),
                )
                chunk_ref[:, 2 * width :] = rest.astype(BF16)

    @pl.when(core_ref[0] == 0)
    def _():
        fill(in_own, in_got)

    @pl.when(core_ref[0] != 0)
    def _():
        fill(out_own, out_got)


def add_chunks(scale, core_ref, chunk_ref, keep_ref, send_ref):
    count, lanes = chunk_ref.shape
    total = chunk_ref[:16, :].astype(F32)
    for start in range(16, count, 16):
        total = total + chunk_ref[start : start + 16, :].astype(F32)
    total = (total[:8] + total[8:]) * scale
    width = keep_ref.shape[1]
    third = width // 3
    first, second, rest = total[:, :width], total[:, width : 2 * width], total[:, 2 * width :]
    last = jnp.concatenate([rest[0:2], rest[2:4], rest[4:6]], axis=1)
    low = jnp.concatenate([first, second[:1]], axis=0)
    high = jnp.concatenate([second[1:], last], axis=0)
    core = core_ref[0]
    keep_ref[...] = jnp.where(core == 0, low, high)
    send_ref[...] = jnp.where(core == 0, high, low)


def place_rows(core_ref, keep_ref, got_ref, qkv_ref, out_ref):
    core = core_ref[0]
    keep, got = keep_ref[...], got_ref[...]
    first = jnp.where(core == 0, keep, got)
    second = jnp.where(core == 0, got, keep)
    qkv_ref[:, : 2 * HK] = first
    qkv_ref[:, 2 * HK :] = second[:, :HK]
    out_ref[...] = second[:, HK:]


SEQ = ("z", "y", "xl")
CHIPS = ("z", "y", "xl", "xh")


def on_device(clips, cotangent, w_qkv_space, w_out_space, w_qkv_time, w_out_time):
    patches, width = clips.shape[2], clips.shape[3]
    frames = lax.axis_size(SEQ)
    chips = lax.axis_size(CHIPS)
    own_patches = patches // frames
    count = patches
    qkv_cols = w_qkv_space.shape[1]
    w_qkv_space, w_out_space = w_qkv_space.T, w_out_space.T
    w_qkv_time, w_out_time = w_qkv_time.T, w_out_time.T
    scale = 1.0 / math.sqrt(count * frames * lax.axis_size(("xh", "c")))
    core = lax.axis_index("c").astype(jnp.int32).reshape(1)
    x = clips.reshape(count, width)
    top = cotangent.reshape(count, width)
    perm = jnp.asarray(permutation(width, chips))
    pairs = [(0, 1), (1, 0)]

    def swap(array):
        return lax.ppermute(array, "c", pairs)

    def exchange(array, axes, parts):
        lanes = array.shape[1]
        array = lax.all_to_all(
            array.reshape(parts, -1, lanes), axes, split_axis=0, concat_axis=0, tiled=True
        )
        return array.reshape(-1, lanes)

    def rows_of(tokens):
        out = call(transpose_rows, [((perm.shape[0], count), BF16)], perm, tokens, flops=10**9)[0]
        return out, swap(out)

    send, qkv_space, attn_space, normed_space = call(
        space_forward,
        [((count, width + HK), BF16), ((count, qkv_cols), BF16), ((count, HK), BF16), ((count, width), BF16)],
        x, top, w_qkv_space, w_out_space, w_out_time, flops=3 * 10**9,
    )
    recv = exchange(send, SEQ, frames)
    back, normed_time, dqkv_time = call(
        functools.partial(time_both, own_patches),
        [((count, width + HK), BF16), ((count, width), BF16), ((count, qkv_cols), BF16)],
        recv, w_qkv_time, flops=5 * 10**9,
    )
    recv = exchange(back, SEQ, frames)
    rows_norm_space = rows_of(normed_space)
    rows_top = rows_of(top)
    rows_norm_time = rows_of(normed_time)
    half = ((count, width), BF16)
    keep, give = call(time_pair, [half, half], core, dqkv_time, recv)
    chunk_shape = ((8 * chips, 2 * width + width // 3), BF16)
    terms_time = call(
        weight_terms, [chunk_shape], core, *rows_norm_time, *rows_top, keep, swap(give),
        flops=2 * 10**9,
    )[0]
    got_time = exchange(terms_time, CHIPS, chips)
    dhidden, dqkv_space, keep, give = call(
        space_backward, [half, ((count, qkv_cols), BF16), half, half],
        core, top, recv, qkv_space, attn_space, w_out_space, flops=3 * 10**9,
    )
    rows_dhidden = rows_of(dhidden)
    terms_space = call(
        weight_terms, [chunk_shape], core, *rows_norm_space, *rows_dhidden, keep, swap(give), flops=2 * 10**9
    )[0]
    got_space = exchange(terms_space, CHIPS, chips)
    grad_clips = call(
        space_finish, [half], x, dhidden, dqkv_space, w_qkv_space, flops=10**9
    )[0]
    mixed = call(mix_out, [half], send, recv, w_out_time, flops=10**9)[0]

    def finish(got):
        rows = width // chips // 2
        own, other = call(
            functools.partial(add_chunks, scale), [((rows, width), F32), ((rows, width), F32)], core, got
        )
        return call(
            place_rows, [((rows, qkv_cols), F32), ((rows, HK), F32)], core, own, swap(other)
        )

    grad_qkv_time, grad_out_time = finish(got_time)
    grad_qkv_space, grad_out_space = finish(got_space)
    return (
        mixed.reshape(clips.shape),
        grad_clips.reshape(clips.shape),
        grad_qkv_space,
        grad_out_space,
        grad_qkv_time,
        grad_out_time,
    )


def solution(mesh):
    fine = Mesh(mesh.devices.reshape(4, 4, 2, 2, 2), ("z", "y", "xl", "xh", "c"))
    tokens = P(("xh", "c"), SEQ, None, None)
    rows = P(("z", "y", "xl", "xh", "c"), None)
    return jax.shard_map(
        on_device,
        mesh=fine,
        in_specs=(tokens, tokens, P(), P(), P(), P()),
        out_specs=(tokens, tokens, rows, rows, rows, rows),
        check_vma=False,
    )
```

```python
import functools
import math

import jax
import jax.numpy as jnp
import numpy as np
from jax import lax
from jax.experimental import pallas as pl
from jax.experimental.pallas import tpu as pltpu
from jax.sharding import Mesh
from jax.sharding import PartitionSpec as P

HEADS = 8
HEAD_DIM = 72
HK = HEADS * HEAD_DIM
EPS = 1e-06
LANES = 128
F32 = jnp.float32
BF16 = jnp.bfloat16


def windows():
    out = []
    for head in range(HEADS):
        low, high = head * HEAD_DIM, (head + 1) * HEAD_DIM
        start = low // LANES * LANES
        stop = min(-(-high // LANES) * LANES, HK)
        out.append((low, high, start, stop))
    return out


def dot_nn(a, b):
    return lax.dot_general(a, b, (((1,), (0,)), ((), ())), preferred_element_type=F32)


def dot_nt(a, b):
    return lax.dot_general(a, b, (((1,), (1,)), ((), ())), preferred_element_type=F32)


def dot_tn(a, b):
    return lax.dot_general(a, b, (((0,), (0,)), ((), ())), preferred_element_type=F32)


def norm_parts(tokens):
    center = tokens - jnp.mean(tokens, axis=-1, keepdims=True)
    spread = jnp.mean(center * center, axis=-1, keepdims=True)
    rate = lax.rsqrt(spread + EPS)
    return center * rate, rate


def norm_back(grad, normed, rate):
    first = jnp.mean(grad, axis=-1, keepdims=True)
    second = jnp.mean(grad * normed, axis=-1, keepdims=True)
    return rate * (grad - first - normed * second)


def split_qkv(qkv):
    return qkv[:, :HK], qkv[:, HK : 2 * HK], qkv[:, 2 * HK :]


class HeadSum:
    def __init__(self):
        self.slabs = [None] * -(-HK // LANES)

    def put(self, head, piece):
        low, high, start, stop = windows()[head]
        for slab in range(start // LANES, -(-stop // LANES)):
            left, right = slab * LANES, min((slab + 1) * LANES, HK)
            part = piece[:, left - start : right - start]
            held = self.slabs[slab]
            if held is not None:
                lane = left + lax.broadcasted_iota(jnp.int32, part.shape, 1)
                part = jnp.where((lane >= low) & (lane < high), part, held)
            self.slabs[slab] = part

    def whole(self, dtype):
        return jnp.concatenate([slab.astype(dtype) for slab in self.slabs], axis=1)


def head_part(array, head):
    low, high, start, stop = windows()[head]
    part = array[:, start:stop]
    lane = start + lax.broadcasted_iota(jnp.int32, part.shape, 1)
    return jnp.where((lane >= low) & (lane < high), part, jnp.zeros_like(part))


def head_window(array, head):
    _, _, start, stop = windows()[head]
    return array[:, start:stop]


def probs_t(query, keys, head, keep):
    scores = dot_nt(head_part(keys, head), head_window(query, head)) * HEAD_DIM ** (-0.5)
    if keep is not None:
        scores = jnp.where(keep, scores, -1e30)
    peak = jnp.max(scores, axis=0, keepdims=True)
    weights = jnp.exp(scores - peak)
    return weights / jnp.sum(weights, axis=0, keepdims=True)


def same_patch(count, patches):
    row = lax.broadcasted_iota(jnp.int32, (count, count), 0)
    col = lax.broadcasted_iota(jnp.int32, (count, count), 1)
    return lax.rem(row, patches) == lax.rem(col, patches)


def space_forward(
    x_hbm, cot_hbm, w_qkv_hbm, w_out_hbm, send_ref, qkv_ref, attn_ref, normed_ref, x_ref, w_qkv_ref, w_out_ref, sems
):
    width = x_ref.shape[1]
    load_x = pltpu.make_async_copy(x_hbm, x_ref, sems.at[0])
    load_x.start()
    loads = []
    for part in range(3):
        rows = pl.ds(part * HK, HK)
        loads.append(pltpu.make_async_copy(w_qkv_hbm.at[rows, :], w_qkv_ref.at[rows, :], sems.at[1 + part]))
    load_out = pltpu.make_async_copy(w_out_hbm, w_out_ref, sems.at[4])
    load_cot = pltpu.make_async_copy(cot_hbm, send_ref.at[:, pl.ds(width, width)], sems.at[5])
    for load in loads + [load_out, load_cot]:
        load.start()
    load_x.wait()
    x = x_ref[...].astype(F32)
    normed = norm_parts(x)[0].astype(BF16)
    normed_ref[...] = normed
    parts = []
    for part, load in enumerate(loads):
        load.wait()
        parts.append(dot_nt(normed, w_qkv_ref[part * HK : (part + 1) * HK, :]).astype(BF16))
    query, keys, values = parts
    qkv_ref[...] = jnp.concatenate(parts, axis=1)
    mix = HeadSum()
    for head in range(HEADS):
        weights = probs_t(query, keys, head, None).astype(BF16)
        mix.put(head, dot_tn(weights, head_window(values, head)))
    attn = mix.whole(BF16)
    attn_ref[...] = attn
    load_out.wait()
    send_ref[:, :width] = (x + dot_nn(attn, w_out_ref[...])).astype(BF16)
    load_cot.wait()


def attention_back(query, keys, values, dmix, keep, forward):
    mix, dq, dk, dv = HeadSum(), HeadSum(), HeadSum(), HeadSum()
    for head in range(HEADS):
        weights = probs_t(query, keys, head, keep)
        rounded = weights.astype(BF16)
        if forward:
            mix.put(head, dot_tn(rounded, head_window(values, head)))
        dprobs = dot_nt(head_part(values, head), head_window(dmix, head)).astype(BF16).astype(F32)
        total = jnp.sum(weights * dprobs, axis=0, keepdims=True)
        dscores = (weights * (dprobs - total) * HEAD_DIM ** (-0.5)).astype(BF16)
        dv.put(head, dot_nn(rounded, head_window(dmix, head)))
        dk.put(head, dot_nn(dscores, head_window(query, head)))
        dq.put(head, dot_tn(dscores, head_window(keys, head)))
    dqkv = jnp.concatenate([dq.whole(BF16), dk.whole(BF16), dv.whole(BF16)], axis=1)
    return (mix.whole(BF16) if forward else None), dqkv


def time_both(
    patches, recv_ref, w_qkv_ref, w_out_ref, back_hbm, normed_hbm, keep_hbm, give_hbm,
    back_ref, normed_ref, keep_ref, give_ref, sems,
):
    width = w_qkv_ref.shape[1]
    hidden = recv_ref[:, :width].astype(F32)
    normed, rate = norm_parts(hidden)
    rounded = normed.astype(BF16)
    normed_ref[...] = rounded
    copies = [pltpu.make_async_copy(normed_ref, normed_hbm, sems.at[0])]
    copies[0].start()
    qkv = dot_nt(rounded, w_qkv_ref[...]).astype(BF16)
    dattn = dot_nt(recv_ref[:, width:], w_out_ref[...]).astype(BF16)
    query, keys, values = split_qkv(qkv)
    keep = same_patch(hidden.shape[0], patches)
    attn, dqkv = attention_back(query, keys, values, dattn, keep, True)
    pair_up(lax.axis_index("c"), dqkv, attn, keep_ref, give_ref)
    back_ref[:, width:] = attn
    for source, target in ((keep_ref, keep_hbm), (give_ref, give_hbm)):
        copies.append(pltpu.make_async_copy(source, target, sems.at[len(copies)]))
        copies[-1].start()
    dnormed = dot_nn(dqkv, w_qkv_ref[...]).astype(BF16).astype(F32)
    back_ref[:, :width] = norm_back(dnormed, normed, rate).astype(BF16)
    copies.append(pltpu.make_async_copy(back_ref, back_hbm, sems.at[3]))
    copies[-1].start()
    for copy in copies:
        copy.wait()


def space_backward(
    cot_ref, recv_ref, qkv_ref, attn_ref, w_out_ref, dhidden_ref, dqkv_ref, keep_ref, send_ref
):
    width = cot_ref.shape[1]
    dhidden = cot_ref[...] + recv_ref[:, :width]
    dhidden_ref[...] = dhidden
    dattn = dot_nt(dhidden, w_out_ref[...]).astype(BF16)
    query, keys, values = split_qkv(qkv_ref[...])
    dqkv = attention_back(query, keys, values, dattn, None, False)[1]
    dqkv_ref[...] = dqkv
    pair_up(lax.axis_index("c"), dqkv, attn_ref[...], keep_ref, send_ref)


def space_finish(x_ref, dhidden_ref, dqkv_ref, w_qkv_ref, grad_ref):
    normed, rate = norm_parts(x_ref[...].astype(F32))
    dnormed = dot_nn(dqkv_ref[...], w_qkv_ref[...]).astype(BF16).astype(F32)
    dres = norm_back(dnormed, normed, rate).astype(BF16)
    grad_ref[...] = dhidden_ref[...] + dres


def call(kernel, outs, *args, flops=0, hbm_in=0, hbm_out=False, vmem_out=False, scratch=(), grant=8):
    size = sum(a.size * a.dtype.itemsize for a in args) + sum(math.prod(shape) * 2 for shape, _ in outs)
    vmem, hbm = pl.BlockSpec(memory_space=pltpu.VMEM), pl.BlockSpec(memory_space=pltpu.HBM)
    args = [
        pltpu.with_memory_space_constraint(arg, pltpu.HBM) if place < hbm_in else arg
        for place, arg in enumerate(args)
    ]
    return pl.pallas_call(
        kernel,
        out_shape=[pltpu.HBM(*out) if hbm_out else pltpu.VMEM(*out) if vmem_out else jax.ShapeDtypeStruct(*out) for out in outs],
        in_specs=[hbm if place < hbm_in else vmem for place in range(len(args))],
        out_specs=[hbm if hbm_out else vmem] * len(outs),
        scratch_shapes=list(scratch),
        compiler_params=pltpu.CompilerParams(vmem_limit_bytes=grant * 1024 * 1024),
        cost_estimate=pl.CostEstimate(flops=flops, bytes_accessed=size, transcendentals=0),
    )(*args)


def permutation(width, chips):
    rows = width // chips
    table = np.zeros((3, chips, 8, width), np.float32)
    for chip in range(chips):
        for lane in range(8):
            table[0, chip, lane, chip * rows + lane] = 1
            table[1, chip, lane, chip * rows + 8 + lane] = 1
        for lane in range(6):
            table[2, chip, lane, chip * rows + 16 + lane % 2] = 1
    return table.reshape(3 * chips * 8, width).astype(jnp.bfloat16)


def transpose_rows(perm_ref, tokens_ref, out_ref):
    width = perm_ref.shape[1]
    tokens = tokens_ref[:, tokens_ref.shape[1] - width :]
    out_ref[...] = dot_nt(perm_ref[...], tokens).astype(BF16)


def stage(from_ref, to_ref, sems):
    rows = from_ref.shape[0] // 4
    copies = []
    for part in range(4):
        block = pl.ds(part * rows, rows)
        copies.append(pltpu.make_async_copy(from_ref.at[block, :], to_ref.at[block, :], sems.at[part]))
        copies[-1].start()
    for copy in copies:
        copy.wait()


def mix_out(send_ref, recv_ref, w_out_ref, mixed_ref):
    width = w_out_ref.shape[1]
    mixed = send_ref[:, :width].astype(F32) + dot_nn(recv_ref[:, width:], w_out_ref[...])
    mixed_ref[...] = mixed.astype(BF16)


def pair_up(core, dqkv, attn, keep_ref, send_ref):
    second = jnp.concatenate([dqkv[:, 2 * HK :], attn], axis=1)
    first = dqkv[:, : 2 * HK]
    keep_ref[...] = jnp.where(core == 0, first, second)
    send_ref[...] = jnp.where(core == 0, second, first)


def weight_terms(in_own, in_got, out_own, out_got, own_ref, got_ref, chunk_ref):
    block = in_own.shape[0] // 3
    low, high = HK // LANES * LANES, -(-HK // LANES) * LANES
    core = lax.axis_index("c")
    width = own_ref.shape[1]
    third = width // 3

    def fill(second_own, second_got):
        for part in range(3):
            rows = pl.ds(part * block, block)
            left = dot_nn(in_own[rows, :], own_ref[:, :high]) + dot_nn(in_got[rows, :], got_ref[:, :high])
            right = dot_nn(second_own[rows, :], own_ref[:, low:]) + dot_nn(
                second_got[rows, :], got_ref[:, low:]
            )
            lane = low + lax.broadcasted_iota(jnp.int32, (block, high - low), 1)
            middle = jnp.where(lane < HK, left[:, low:], right[:, : high - low])
            whole = jnp.concatenate([left[:, :low], middle, right[:, high - low :]], axis=1)
            if part < 2:
                chunk_ref[:, part * width : (part + 1) * width] = whole.astype(BF16)
            else:
                row = lax.rem(lax.broadcasted_iota(jnp.int32, (block, third), 0), 8)
                rest = jnp.where(
                    row < 2,
                    whole[:, :third],
                    jnp.where(row < 4, whole[:, third : 2 * third], whole[:, 2 * third :]),
                )
                chunk_ref[:, 2 * width :] = rest.astype(BF16)

    @pl.when(core == 0)
    def _():
        fill(in_own, in_got)

    @pl.when(core != 0)
    def _():
        fill(out_own, out_got)


def add_chunks(scale, chunk_ref, keep_ref, send_ref):
    count, lanes = chunk_ref.shape
    total = chunk_ref[:16, :].astype(F32)
    for start in range(16, count, 16):
        total = total + chunk_ref[start : start + 16, :].astype(F32)
    total = (total[:8] + total[8:]) * scale
    width = keep_ref.shape[1]
    third = width // 3
    first, second, rest = total[:, :width], total[:, width : 2 * width], total[:, 2 * width :]
    last = jnp.concatenate([rest[0:2], rest[2:4], rest[4:6]], axis=1)
    low = jnp.concatenate([first, second[:1]], axis=0)
    high = jnp.concatenate([second[1:], last], axis=0)
    core = lax.axis_index("c")
    keep_ref[...] = jnp.where(core == 0, low, high)
    send_ref[...] = jnp.where(core == 0, high, low)


def place_rows(keep_ref, got_ref, qkv_ref, out_ref):
    core = lax.axis_index("c")
    keep, got = keep_ref[...], got_ref[...]
    first = jnp.where(core == 0, keep, got)
    second = jnp.where(core == 0, got, keep)
    qkv_ref[:, : 2 * HK] = first
    qkv_ref[:, 2 * HK :] = second[:, :HK]
    out_ref[...] = second[:, HK:]


SEQ = ("z", "y", "xl")
CHIPS = ("z", "y", "xl", "xh")


def on_device(clips, cotangent, w_qkv_space, w_out_space, w_qkv_time, w_out_time):
    patches, width = clips.shape[2], clips.shape[3]
    frames = lax.axis_size(SEQ)
    chips = lax.axis_size(CHIPS)
    own_patches = patches // frames
    count = patches
    qkv_cols = w_qkv_space.shape[1]
    w_qkv_space, w_out_space = w_qkv_space.T, w_out_space.T
    w_qkv_time, w_out_time = w_qkv_time.T, w_out_time.T
    scale = 1.0 / math.sqrt(count * frames * lax.axis_size(("xh", "c")))
    x = clips.reshape(count, width)
    top = cotangent.reshape(count, width)
    perm = jnp.asarray(permutation(width, chips))
    pairs = [(0, 1), (1, 0)]

    def swap(array):
        return lax.ppermute(array, "c", pairs)

    def exchange(array, axes, parts):
        lanes = array.shape[1]
        array = lax.all_to_all(
            array.reshape(parts, -1, lanes), axes, split_axis=0, concat_axis=0, tiled=True
        )
        return array.reshape(-1, lanes)

    def rows_of(tokens):
        out = call(transpose_rows, [((perm.shape[0], count), BF16)], perm, tokens, flops=10**9)[0]
        return out, swap(out)

    half = ((count, width), BF16)
    send, qkv_space, attn_space, normed_space = call(
        space_forward,
        [((count, 2 * width), BF16), ((count, qkv_cols), BF16), ((count, HK), BF16), half],
        x, top, w_qkv_space, w_out_space,
        flops=3 * 10**9,
        hbm_in=4,
        scratch=[
            pltpu.VMEM((count, width), BF16),
            pltpu.VMEM((qkv_cols, width), BF16),
            pltpu.VMEM((HK, width), BF16),
            pltpu.SemaphoreType.DMA((6,)),
        ],
        grant=16,
    )
    recv = exchange(send, SEQ, frames)
    back, normed_time, keep, give = call(
        functools.partial(time_both, own_patches),
        [((count, width + HK), BF16), half, half, half],
        recv, w_qkv_time, w_out_time,
        flops=5 * 10**9,
        hbm_out=True,
        scratch=[
            pltpu.VMEM((count, width + HK), BF16),
            pltpu.VMEM((count, width), BF16),
            pltpu.VMEM((count, width), BF16),
            pltpu.VMEM((count, width), BF16),
            pltpu.SemaphoreType.DMA((4,)),
        ],
        grant=16,
    )
    chunk_shape = ((8 * chips, 2 * width + width // 3), BF16)
    got_pair = swap(give)
    rows_norm_time = rows_of(normed_time)
    rows_top = rows_of(recv)
    terms_time = call(
        weight_terms, [chunk_shape], *rows_norm_time, *rows_top, keep, got_pair, flops=2 * 10**9
    )[0]
    recv = exchange(back, SEQ, frames)
    recv, terms_time = lax.optimization_barrier((recv, terms_time))
    got_time = exchange(terms_time, CHIPS, chips)
    rows_norm_space = rows_of(normed_space)
    dhidden, dqkv_space, keep, give = call(
        space_backward, [half, ((count, qkv_cols), BF16), half, half],
        top, recv, qkv_space, attn_space, w_out_space, flops=3 * 10**9,
    )
    got_pair = swap(give)
    rows_dhidden = rows_of(dhidden)
    terms_space = call(
        weight_terms, [chunk_shape], *rows_norm_space, *rows_dhidden, keep, got_pair, flops=2 * 10**9
    )[0]
    grad_clips = call(
        space_finish, [half], x, dhidden, dqkv_space, w_qkv_space, flops=10**9
    )[0]
    mixed = call(mix_out, [half], send, recv, w_out_time, flops=10**9)[0]
    terms_space, grad_clips, mixed, got_time = lax.optimization_barrier(
        (terms_space, grad_clips, mixed, got_time)
    )
    terms_space = call(
        stage, [chunk_shape], terms_space, hbm_in=1, vmem_out=True, scratch=[pltpu.SemaphoreType.DMA((4,))]
    )[0]
    got_space = exchange(terms_space, CHIPS, chips)
    got_time, got_space = lax.optimization_barrier((got_time, got_space))

    def finish(got):
        rows = width // chips // 2
        own, other = call(
            functools.partial(add_chunks, scale), [((rows, width), F32), ((rows, width), F32)], got
        )
        return call(
            place_rows, [((rows, qkv_cols), F32), ((rows, HK), F32)], own, swap(other)
        )

    grad_qkv_time, grad_out_time = finish(got_time)
    grad_qkv_space, grad_out_space = finish(got_space)
    return (
        mixed.reshape(clips.shape),
        grad_clips.reshape(clips.shape),
        grad_qkv_space,
        grad_out_space,
        grad_qkv_time,
        grad_out_time,
    )


def solution(mesh):
    fine = Mesh(mesh.devices.reshape(4, 4, 2, 2, 2), ("z", "y", "xl", "xh", "c"))
    tokens = P(("xh", "c"), SEQ, None, None)
    rows = P(("z", "y", "xl", "xh", "c"), None)
    return jax.shard_map(
        on_device,
        mesh=fine,
        in_specs=(tokens, tokens, P(), P(), P(), P()),
        out_specs=(tokens, tokens, rows, rows, rows, rows),
        check_vma=False,
    )
```

```python
import functools
import math

import jax
import jax.numpy as jnp
import numpy as np
from jax import lax
from jax.experimental import pallas as pl
from jax.experimental.pallas import tpu as pltpu
from jax.sharding import Mesh
from jax.sharding import PartitionSpec as P

HEADS = 8
HEAD_DIM = 72
HK = HEADS * HEAD_DIM
EPS = 1e-06
LANES = 128
F32 = jnp.float32
BF16 = jnp.bfloat16


def windows():
    out = []
    for head in range(HEADS):
        low, high = head * HEAD_DIM, (head + 1) * HEAD_DIM
        start = low // LANES * LANES
        stop = min(-(-high // LANES) * LANES, HK)
        out.append((low, high, start, stop))
    return out


def dot_nn(a, b):
    return lax.dot_general(a, b, (((1,), (0,)), ((), ())), preferred_element_type=F32)


def dot_nt(a, b):
    return lax.dot_general(a, b, (((1,), (1,)), ((), ())), preferred_element_type=F32)


def dot_tn(a, b):
    return lax.dot_general(a, b, (((0,), (0,)), ((), ())), preferred_element_type=F32)


def norm_parts(tokens):
    center = tokens - jnp.mean(tokens, axis=-1, keepdims=True)
    spread = jnp.mean(center * center, axis=-1, keepdims=True)
    rate = lax.rsqrt(spread + EPS)
    return center * rate, rate


def norm_back(grad, normed, rate):
    first = jnp.mean(grad, axis=-1, keepdims=True)
    second = jnp.mean(grad * normed, axis=-1, keepdims=True)
    return rate * (grad - first - normed * second)


def split_qkv(qkv):
    return qkv[:, :HK], qkv[:, HK : 2 * HK], qkv[:, 2 * HK :]


class HeadSum:
    def __init__(self):
        self.slabs = [None] * -(-HK // LANES)

    def put(self, head, piece):
        low, high, start, stop = windows()[head]
        for slab in range(start // LANES, -(-stop // LANES)):
            left, right = slab * LANES, min((slab + 1) * LANES, HK)
            part = piece[:, left - start : right - start]
            held = self.slabs[slab]
            if held is not None:
                lane = left + lax.broadcasted_iota(jnp.int32, part.shape, 1)
                part = jnp.where((lane >= low) & (lane < high), part, held)
            self.slabs[slab] = part

    def whole(self, dtype):
        return jnp.concatenate([slab.astype(dtype) for slab in self.slabs], axis=1)


def head_part(array, head):
    low, high, start, stop = windows()[head]
    part = array[:, start:stop]
    lane = start + lax.broadcasted_iota(jnp.int32, part.shape, 1)
    return jnp.where((lane >= low) & (lane < high), part, jnp.zeros_like(part))


def head_window(array, head):
    _, _, start, stop = windows()[head]
    return array[:, start:stop]


def probs_t(query, keys, head, keep):
    scores = dot_nt(head_part(keys, head), head_window(query, head)) * HEAD_DIM ** (-0.5)
    if keep is not None:
        scores = jnp.where(keep, scores, -1e30)
    peak = jnp.max(scores, axis=0, keepdims=True)
    weights = jnp.exp(scores - peak)
    return weights / jnp.sum(weights, axis=0, keepdims=True)


def same_patch(count, patches):
    row = lax.broadcasted_iota(jnp.int32, (count, count), 0)
    col = lax.broadcasted_iota(jnp.int32, (count, count), 1)
    return lax.rem(row, patches) == lax.rem(col, patches)


def space_forward(
    x_hbm, cot_hbm, w_qkv_hbm, w_out_hbm, send_ref, qkv_hbm, attn_hbm, normed_hbm,
    x_ref, w_qkv_ref, w_out_ref, qkv_ref, attn_ref, normed_ref, sems,
):
    width = x_ref.shape[1]
    load_x = pltpu.make_async_copy(x_hbm, x_ref, sems.at[0])
    load_x.start()
    loads = []
    for part in range(3):
        rows = pl.ds(part * HK, HK)
        loads.append(pltpu.make_async_copy(w_qkv_hbm.at[rows, :], w_qkv_ref.at[rows, :], sems.at[1 + part]))
    load_out = pltpu.make_async_copy(w_out_hbm, w_out_ref, sems.at[4])
    load_cot = pltpu.make_async_copy(cot_hbm, send_ref.at[:, pl.ds(width, width)], sems.at[5])
    for load in loads + [load_out, load_cot]:
        load.start()
    load_x.wait()
    x = x_ref[...].astype(F32)
    normed = norm_parts(x)[0].astype(BF16)
    normed_ref[...] = normed
    store_normed = pltpu.make_async_copy(normed_ref, normed_hbm, sems.at[6])
    store_normed.start()
    parts = []
    for part, load in enumerate(loads):
        load.wait()
        parts.append(dot_nt(normed, w_qkv_ref[part * HK : (part + 1) * HK, :]).astype(BF16))
    query, keys, values = parts
    qkv_ref[...] = jnp.concatenate(parts, axis=1)
    store_qkv = pltpu.make_async_copy(qkv_ref, qkv_hbm, sems.at[7])
    store_qkv.start()
    mix = HeadSum()
    for head in range(HEADS):
        weights = probs_t(query, keys, head, None).astype(BF16)
        mix.put(head, dot_tn(weights, head_window(values, head)))
    attn = mix.whole(BF16)
    attn_ref[...] = attn
    store_attn = pltpu.make_async_copy(attn_ref, attn_hbm, sems.at[8])
    store_attn.start()
    load_out.wait()
    send_ref[:, :width] = (x + dot_nn(attn, w_out_ref[...])).astype(BF16)
    for copy in (load_cot, store_normed, store_qkv, store_attn):
        copy.wait()


def attention_back(query, keys, values, dmix, keep, forward):
    mix, dq, dk, dv = HeadSum(), HeadSum(), HeadSum(), HeadSum()
    for head in range(HEADS):
        weights = probs_t(query, keys, head, keep)
        rounded = weights.astype(BF16)
        if forward:
            mix.put(head, dot_tn(rounded, head_window(values, head)))
        dprobs = dot_nt(head_part(values, head), head_window(dmix, head)).astype(BF16).astype(F32)
        total = jnp.sum(weights * dprobs, axis=0, keepdims=True)
        dscores = (weights * (dprobs - total) * HEAD_DIM ** (-0.5)).astype(BF16)
        dv.put(head, dot_nn(rounded, head_window(dmix, head)))
        dk.put(head, dot_nn(dscores, head_window(query, head)))
        dq.put(head, dot_tn(dscores, head_window(keys, head)))
    dqkv = jnp.concatenate([dq.whole(BF16), dk.whole(BF16), dv.whole(BF16)], axis=1)
    return (mix.whole(BF16) if forward else None), dqkv


def time_both(
    patches, recv_ref, w_qkv_ref, w_out_ref, back_hbm, normed_hbm, top_hbm, keep_hbm, give_hbm,
    back_ref, normed_ref, keep_ref, give_ref, sems,
):
    width = w_qkv_ref.shape[1]
    hidden = recv_ref[:, :width].astype(F32)
    normed, rate = norm_parts(hidden)
    rounded = normed.astype(BF16)
    normed_ref[...] = rounded
    copies = [
        pltpu.make_async_copy(normed_ref, normed_hbm, sems.at[0]),
        pltpu.make_async_copy(recv_ref.at[:, pl.ds(width, width)], top_hbm, sems.at[1]),
    ]
    for copy in copies:
        copy.start()
    qkv = dot_nt(rounded, w_qkv_ref[...]).astype(BF16)
    dattn = dot_nt(recv_ref[:, width:], w_out_ref[...]).astype(BF16)
    query, keys, values = split_qkv(qkv)
    keep = same_patch(hidden.shape[0], patches)
    attn, dqkv = attention_back(query, keys, values, dattn, keep, True)
    pair_up(lax.axis_index("c"), dqkv, attn, keep_ref, give_ref)
    back_ref[:, width:] = attn
    for source, target in ((keep_ref, keep_hbm), (give_ref, give_hbm)):
        copies.append(pltpu.make_async_copy(source, target, sems.at[len(copies)]))
        copies[-1].start()
    dnormed = dot_nn(dqkv, w_qkv_ref[...]).astype(BF16).astype(F32)
    back_ref[:, :width] = norm_back(dnormed, normed, rate).astype(BF16)
    copies.append(pltpu.make_async_copy(back_ref, back_hbm, sems.at[4]))
    copies[-1].start()
    for copy in copies:
        copy.wait()


def space_backward(
    cot_ref, recv_ref, qkv_ref, attn_ref, w_out_ref, dhidden_ref, dqkv_ref, keep_ref, send_ref
):
    width = cot_ref.shape[1]
    dhidden = cot_ref[...] + recv_ref[:, :width]
    dhidden_ref[...] = dhidden
    dattn = dot_nt(dhidden, w_out_ref[...]).astype(BF16)
    query, keys, values = split_qkv(qkv_ref[...])
    dqkv = attention_back(query, keys, values, dattn, None, False)[1]
    dqkv_ref[...] = dqkv
    pair_up(lax.axis_index("c"), dqkv, attn_ref[...], keep_ref, send_ref)


def space_finish(x_ref, dhidden_ref, dqkv_ref, w_qkv_ref, grad_ref):
    normed, rate = norm_parts(x_ref[...].astype(F32))
    dnormed = dot_nn(dqkv_ref[...], w_qkv_ref[...]).astype(BF16).astype(F32)
    dres = norm_back(dnormed, normed, rate).astype(BF16)
    grad_ref[...] = dhidden_ref[...] + dres


def call(kernel, outs, *args, flops=0, hbm_in=0, hbm_out=(), scratch=(), grant=8):
    size = sum(a.size * a.dtype.itemsize for a in args) + sum(math.prod(shape) * 2 for shape, _ in outs)
    vmem, hbm = pl.BlockSpec(memory_space=pltpu.VMEM), pl.BlockSpec(memory_space=pltpu.HBM)
    args = [
        pltpu.with_memory_space_constraint(arg, pltpu.HBM) if place < hbm_in else arg
        for place, arg in enumerate(args)
    ]
    return pl.pallas_call(
        kernel,
        out_shape=[
            pltpu.HBM(*out) if place in hbm_out else jax.ShapeDtypeStruct(*out)
            for place, out in enumerate(outs)
        ],
        in_specs=[hbm if place < hbm_in else vmem for place in range(len(args))],
        out_specs=[hbm if place in hbm_out else vmem for place in range(len(outs))],
        scratch_shapes=list(scratch),
        compiler_params=pltpu.CompilerParams(vmem_limit_bytes=grant * 1024 * 1024),
        cost_estimate=pl.CostEstimate(flops=flops, bytes_accessed=size, transcendentals=0),
    )(*args)


def chunk_rows(chunks, rows, parts):
    table = np.zeros((3, chunks, parts, 8, parts, chunks * rows), np.float32)
    for chunk in range(chunks):
        for part in range(parts):
            for lane in range(8):
                table[0, chunk, part, lane, part, chunk * rows + lane] = 1
                table[1, chunk, part, lane, part, chunk * rows + 8 + lane] = 1
            for lane in range(6):
                table[2, chunk, part, lane, part, chunk * rows + 16 + lane % 2] = 1
    return table.reshape(3 * chunks * parts * 8, parts * chunks * rows).astype(jnp.bfloat16)


def mix_out(send_ref, recv_ref, w_out_ref, mixed_ref):
    width = w_out_ref.shape[1]
    mixed = send_ref[:, :width].astype(F32) + dot_nn(recv_ref[:, width:], w_out_ref[...])
    mixed_ref[...] = mixed.astype(BF16)


def pair_up(core, dqkv, attn, keep_ref, send_ref):
    second = jnp.concatenate([dqkv[:, 2 * HK :], attn], axis=1)
    first = dqkv[:, : 2 * HK]
    keep_ref[...] = jnp.where(core == 0, first, second)
    send_ref[...] = jnp.where(core == 0, second, first)


def weight_terms(lines, in_own, in_got, out_own, out_got, own_ref, got_ref, term_ref, total_ref):
    width = own_ref.shape[1]
    low, high = HK // LANES * LANES, -(-HK // LANES) * LANES
    step = width // 3
    rows = width // (lines * lines)
    core = lax.axis_index("c")

    def product(one, two, left, right):
        return dot_tn(one, own_ref[:, left:right]) + dot_tn(two, got_ref[:, left:right])

    def place(order):
        for first in range(0, lines * lines, 2):
            pair = [total_ref[pl.ds(order(block) * rows, rows), :] for block in (first, first + 1)]
            term_ref[pl.ds(first * rows, 2 * rows), :] = jnp.concatenate(pair, axis=0).astype(BF16)

    @pl.when(core == 0)
    def _():
        for start in range(0, width, step):
            block = slice(start, start + step)
            total_ref[block, :] = product(in_own[:, block], in_got[:, block], 0, width)
        place(lambda block: block)

    @pl.when(core != 0)
    def _():
        for start in range(0, width, step):
            block = slice(start, start + step)
            left = product(in_own[:, block], in_got[:, block], 0, high)
            right = product(out_own[:, block], out_got[:, block], low, width)
            lane = low + lax.broadcasted_iota(jnp.int32, (step, high - low), 1)
            total_ref[block, :low] = left[:, :low]
            total_ref[block, low:high] = jnp.where(lane < HK, left[:, low:], right[:, : high - low])
            total_ref[block, high:] = right[:, high - low :]
        place(lambda block: block % lines * lines + block // lines)


def add_lines(lines, table_ref, time_ref, space_ref, chunk_ref):
    width = time_ref.shape[1]
    third = width // 3
    sums = []
    for ref in (time_ref, space_ref):
        rows = ref.shape[0] // lines
        total = ref[:rows, :].astype(F32)
        for line in range(1, lines):
            total = total + ref[line * rows : (line + 1) * rows, :].astype(F32)
        sums.append(total.astype(BF16))
    sums = jnp.concatenate(sums, axis=0)
    block = table_ref.shape[0] // 3
    for part in range(3):
        whole = dot_nn(table_ref[part * block : (part + 1) * block, :], sums)
        if part < 2:
            chunk_ref[:, part * width : (part + 1) * width] = whole.astype(BF16)
        else:
            row = lax.rem(lax.broadcasted_iota(jnp.int32, (block, third), 0), 8)
            rest = jnp.where(
                row < 2,
                whole[:, :third],
                jnp.where(row < 4, whole[:, third : 2 * third], whole[:, 2 * third :]),
            )
            chunk_ref[:, 2 * width :] = rest.astype(BF16)


def add_chunks(scale, chunk_ref, keep_ref, send_ref):
    count, lanes = chunk_ref.shape
    total = chunk_ref[:16, :].astype(F32)
    for start in range(16, count, 16):
        total = total + chunk_ref[start : start + 16, :].astype(F32)
    total = total * scale
    width = lanes // 7 * 3
    third = width // 3
    core = lax.axis_index("c")
    for part in range(2):
        held = total[8 * part : 8 * part + 8]
        first, second, rest = held[:, :width], held[:, width : 2 * width], held[:, 2 * width :]
        last = jnp.concatenate([rest[0:2], rest[2:4], rest[4:6]], axis=1)
        low = jnp.concatenate([first, second[:1]], axis=0)
        high = jnp.concatenate([second[1:], last], axis=0)
        keep_ref[part] = jnp.where(core == 0, low, high)
        send_ref[part] = jnp.where(core == 0, high, low)


def place_rows(keep_ref, got_ref, qkv_time_ref, out_time_ref, qkv_space_ref, out_space_ref):
    core = lax.axis_index("c")
    for part, (qkv_ref, out_ref) in enumerate(
        ((qkv_time_ref, out_time_ref), (qkv_space_ref, out_space_ref))
    ):
        keep, got = keep_ref[part], got_ref[part]
        first = jnp.where(core == 0, keep, got)
        second = jnp.where(core == 0, got, keep)
        qkv_ref[:, : 2 * HK] = first
        qkv_ref[:, 2 * HK :] = second[:, :HK]
        out_ref[...] = second[:, HK:]


SEQ = ("z", "y", "xl")
ALL = ("z", "y", "xl", "xh", "c")
SIDE = 4


def device(z, y, x, core):
    return ((z * SIDE + y) * SIDE + x) * 2 + core


def line_groups():
    side = range(SIDE)
    groups = [[device(z, y, x, 0) for z in side] for y in side for x in side]
    return groups + [[device(z, y, x, 1) for y in side] for z in side for x in side]


def plane_groups():
    side = range(SIDE)
    groups = [[device(z, y, x, 0) for y in side for x in side] for z in side]
    return groups + [[device(z, y, x, 1) for z in side for x in side] for y in side]


def on_device(clips, cotangent, w_qkv_space, w_out_space, w_qkv_time, w_out_time):
    patches, width = clips.shape[2], clips.shape[3]
    frames = lax.axis_size(SEQ)
    own_patches = patches // frames
    count = patches
    qkv_cols = w_qkv_space.shape[1]
    w_qkv_space, w_out_space = w_qkv_space.T, w_out_space.T
    w_qkv_time, w_out_time = w_qkv_time.T, w_out_time.T
    scale = 1.0 / math.sqrt(count * frames * lax.axis_size(("xh", "c")))
    x = clips.reshape(count, width)
    top = cotangent.reshape(count, width)
    plane = SIDE * SIDE
    rows = width // (plane * SIDE)
    table = jnp.asarray(chunk_rows(plane, rows, 2))
    half = ((count, width), BF16)
    term = ((width, width), BF16)

    def swap(array):
        return lax.ppermute(array, "c", [(0, 1), (1, 0)])

    def exchange(array, axes, parts, groups=None):
        lanes = array.shape[1]
        array = lax.all_to_all(
            array.reshape(parts, -1, lanes),
            axes,
            split_axis=0,
            concat_axis=0,
            tiled=True,
            axis_index_groups=groups,
        )
        return array.reshape(-1, lanes)

    def terms(*args):
        return call(
            functools.partial(weight_terms, SIDE),
            [term],
            *args,
            flops=2 * 10**9,
            scratch=[pltpu.VMEM((width, width), F32)],
            grant=16,
        )[0]

    def buffers(*shapes):
        return [pltpu.VMEM(*shape) for shape in shapes]

    qkv = ((count, qkv_cols), BF16)
    mix = ((count, HK), BF16)
    send, qkv_space, attn_space, normed_space = call(
        space_forward,
        [((count, 2 * width), BF16), qkv, mix, half],
        x, top, w_qkv_space, w_out_space,
        flops=3 * 10**9,
        hbm_in=4,
        hbm_out=(1, 2, 3),
        scratch=buffers(half, ((qkv_cols, width), BF16), ((HK, width), BF16), qkv, mix, half)
        + [pltpu.SemaphoreType.DMA((9,))],
        grant=16,
    )
    recv = exchange(send, SEQ, frames)
    pack = ((count, width + HK), BF16)
    back, normed_time, top_time, keep, give = call(
        functools.partial(time_both, own_patches),
        [pack, half, half, half, half],
        recv, w_qkv_time, w_out_time,
        flops=5 * 10**9,
        hbm_out=(0, 1, 2, 3, 4),
        scratch=buffers(pack, half, half, half) + [pltpu.SemaphoreType.DMA((5,))],
        grant=16,
    )
    terms_time = terms(
        normed_time, swap(normed_time), top_time, swap(top_time), keep, swap(give)
    )
    recv = exchange(back, SEQ, frames)
    recv, terms_time = lax.optimization_barrier((recv, terms_time))
    got_time = exchange(terms_time, ALL, SIDE, line_groups())
    dhidden, dqkv_space, keep, give = call(
        space_backward, [half, qkv, half, half],
        top, recv, qkv_space, attn_space, w_out_space, flops=3 * 10**9,
    )
    terms_space = terms(
        normed_space, swap(normed_space), dhidden, swap(dhidden), keep, swap(give)
    )
    got_space = exchange(terms_space, ALL, SIDE, line_groups())
    grad_clips = call(
        space_finish, [half], x, dhidden, dqkv_space, w_qkv_space, flops=10**9
    )[0]
    mixed = call(mix_out, [half], send, recv, w_out_time, flops=10**9)[0]
    chunks = call(
        functools.partial(add_lines, SIDE),
        [((plane * 16, 2 * width + width // 3), BF16)],
        table, got_time, got_space,
        flops=10**9,
    )[0]
    chunks, grad_clips, mixed = lax.optimization_barrier((chunks, grad_clips, mixed))
    chunks = exchange(chunks, ALL, plane, plane_groups())
    own_rows = ((2, rows // 2, width), F32)
    own, other = call(functools.partial(add_chunks, scale), [own_rows, own_rows], chunks)
    grad_qkv = ((rows // 2, qkv_cols), F32)
    grad_out = ((rows // 2, HK), F32)
    grad_qkv_time, grad_out_time, grad_qkv_space, grad_out_space = call(
        place_rows, [grad_qkv, grad_out, grad_qkv, grad_out], own, swap(other)
    )
    return (
        mixed.reshape(clips.shape),
        grad_clips.reshape(clips.shape),
        grad_qkv_space,
        grad_out_space,
        grad_qkv_time,
        grad_out_time,
    )


def solution(mesh):
    fine = Mesh(mesh.devices.reshape(4, 4, 2, 2, 2), ("z", "y", "xl", "xh", "c"))
    tokens = P(("xh", "c"), SEQ, None, None)
    rows = P(("z", "y", "xl", "xh", "c"), None)
    return jax.shard_map(
        on_device,
        mesh=fine,
        in_specs=(tokens, tokens, P(), P(), P(), P()),
        out_specs=(tokens, tokens, rows, rows, rows, rows),
        check_vma=False,
    )
```

```python
import functools
import math

import jax
import jax.numpy as jnp
import numpy as np
from jax import lax
from jax.experimental import pallas as pl
from jax.experimental.pallas import tpu as pltpu
from jax.sharding import Mesh
from jax.sharding import PartitionSpec as P

HEADS = 8
HEAD_DIM = 72
HK = HEADS * HEAD_DIM
EPS = 1e-06
LANES = 128
F32 = jnp.float32
BF16 = jnp.bfloat16


def windows():
    out = []
    for head in range(HEADS):
        low, high = head * HEAD_DIM, (head + 1) * HEAD_DIM
        start = low // LANES * LANES
        stop = min(-(-high // LANES) * LANES, HK)
        out.append((low, high, start, stop))
    return out


def dot_nn(a, b):
    return lax.dot_general(a, b, (((1,), (0,)), ((), ())), preferred_element_type=F32)


def dot_nt(a, b):
    return lax.dot_general(a, b, (((1,), (1,)), ((), ())), preferred_element_type=F32)


def dot_tn(a, b):
    return lax.dot_general(a, b, (((0,), (0,)), ((), ())), preferred_element_type=F32)


def norm_parts(tokens):
    center = tokens - jnp.mean(tokens, axis=-1, keepdims=True)
    spread = jnp.mean(center * center, axis=-1, keepdims=True)
    rate = lax.rsqrt(spread + EPS)
    return center * rate, rate


def norm_back(grad, normed, rate):
    first = jnp.mean(grad, axis=-1, keepdims=True)
    second = jnp.mean(grad * normed, axis=-1, keepdims=True)
    return rate * (grad - first - normed * second)


def split_qkv(qkv):
    return qkv[:, :HK], qkv[:, HK : 2 * HK], qkv[:, 2 * HK :]


class HeadSum:
    def __init__(self):
        self.slabs = [None] * -(-HK // LANES)

    def put(self, head, piece):
        low, high, start, stop = windows()[head]
        for slab in range(start // LANES, -(-stop // LANES)):
            left, right = slab * LANES, min((slab + 1) * LANES, HK)
            part = piece[:, left - start : right - start]
            held = self.slabs[slab]
            if held is not None:
                lane = left + lax.broadcasted_iota(jnp.int32, part.shape, 1)
                part = jnp.where((lane >= low) & (lane < high), part, held)
            self.slabs[slab] = part

    def whole(self, dtype):
        return jnp.concatenate([slab.astype(dtype) for slab in self.slabs], axis=1)


def head_part(array, head):
    low, high, start, stop = windows()[head]
    part = array[:, start:stop]
    lane = start + lax.broadcasted_iota(jnp.int32, part.shape, 1)
    return jnp.where((lane >= low) & (lane < high), part, jnp.zeros_like(part))


def head_window(array, head):
    _, _, start, stop = windows()[head]
    return array[:, start:stop]


def probs_t(query, keys, head, keep):
    scores = dot_nt(head_part(keys, head), head_window(query, head)) * HEAD_DIM ** (-0.5)
    if keep is not None:
        scores = jnp.where(keep, scores, -1e30)
    peak = jnp.max(scores, axis=0, keepdims=True)
    weights = jnp.exp(scores - peak)
    return weights / jnp.sum(weights, axis=0, keepdims=True)


def same_patch(count, patches):
    row = lax.broadcasted_iota(jnp.int32, (count, count), 0)
    col = lax.broadcasted_iota(jnp.int32, (count, count), 1)
    return lax.rem(row, patches) == lax.rem(col, patches)


def space_forward(
    x_hbm, cot_hbm, w_qkv_hbm, w_out_hbm, send_ref, qkv_hbm, attn_hbm, normed_hbm,
    x_ref, w_qkv_ref, w_out_ref, qkv_ref, attn_ref, normed_ref, sems,
):
    width = x_ref.shape[1]
    load_x = pltpu.make_async_copy(x_hbm, x_ref, sems.at[0])
    load_x.start()
    loads = []
    for part in range(3):
        rows = pl.ds(part * HK, HK)
        loads.append(pltpu.make_async_copy(w_qkv_hbm.at[rows, :], w_qkv_ref.at[rows, :], sems.at[1 + part]))
    load_out = pltpu.make_async_copy(w_out_hbm, w_out_ref, sems.at[4])
    load_cot = pltpu.make_async_copy(cot_hbm, send_ref.at[:, pl.ds(width, width)], sems.at[5])
    for load in loads + [load_out, load_cot]:
        load.start()
    load_x.wait()
    x = x_ref[...].astype(F32)
    normed = norm_parts(x)[0].astype(BF16)
    normed_ref[...] = normed
    store_normed = pltpu.make_async_copy(normed_ref, normed_hbm, sems.at[6])
    store_normed.start()
    parts = []
    for part, load in enumerate(loads):
        load.wait()
        parts.append(dot_nt(normed, w_qkv_ref[part * HK : (part + 1) * HK, :]).astype(BF16))
    query, keys, values = parts
    qkv_ref[...] = jnp.concatenate(parts, axis=1)
    store_qkv = pltpu.make_async_copy(qkv_ref, qkv_hbm, sems.at[7])
    store_qkv.start()
    mix = HeadSum()
    for head in range(HEADS):
        weights = probs_t(query, keys, head, None).astype(BF16)
        mix.put(head, dot_tn(weights, head_window(values, head)))
    attn = mix.whole(BF16)
    attn_ref[...] = attn
    store_attn = pltpu.make_async_copy(attn_ref, attn_hbm, sems.at[8])
    store_attn.start()
    load_out.wait()
    send_ref[:, :width] = (x + dot_nn(attn, w_out_ref[...])).astype(BF16)
    for copy in (load_cot, store_normed, store_qkv, store_attn):
        copy.wait()


def attention_back(query, keys, values, dmix, keep, forward):
    mix, dq, dk, dv = HeadSum(), HeadSum(), HeadSum(), HeadSum()
    for head in range(HEADS):
        weights = probs_t(query, keys, head, keep)
        rounded = weights.astype(BF16)
        if forward:
            mix.put(head, dot_tn(rounded, head_window(values, head)))
        dprobs = dot_nt(head_part(values, head), head_window(dmix, head)).astype(BF16).astype(F32)
        total = jnp.sum(weights * dprobs, axis=0, keepdims=True)
        dscores = (weights * (dprobs - total) * HEAD_DIM ** (-0.5)).astype(BF16)
        dv.put(head, dot_nn(rounded, head_window(dmix, head)))
        dk.put(head, dot_nn(dscores, head_window(query, head)))
        dq.put(head, dot_tn(dscores, head_window(keys, head)))
    dqkv = jnp.concatenate([dq.whole(BF16), dk.whole(BF16), dv.whole(BF16)], axis=1)
    return (mix.whole(BF16) if forward else None), dqkv


def time_both(
    patches, recv_ref, w_qkv_ref, w_out_ref, back_hbm, normed_hbm, top_hbm, keep_hbm, give_hbm,
    back_ref, normed_ref, keep_ref, give_ref, sems,
):
    width = w_qkv_ref.shape[1]
    hidden = recv_ref[:, :width].astype(F32)
    normed, rate = norm_parts(hidden)
    rounded = normed.astype(BF16)
    normed_ref[...] = rounded
    copies = [
        pltpu.make_async_copy(normed_ref, normed_hbm, sems.at[0]),
        pltpu.make_async_copy(recv_ref.at[:, pl.ds(width, width)], top_hbm, sems.at[1]),
    ]
    for copy in copies:
        copy.start()
    qkv = dot_nt(rounded, w_qkv_ref[...]).astype(BF16)
    dattn = dot_nt(recv_ref[:, width:], w_out_ref[...]).astype(BF16)
    query, keys, values = split_qkv(qkv)
    keep = same_patch(hidden.shape[0], patches)
    attn, dqkv = attention_back(query, keys, values, dattn, keep, True)
    pair_up(lax.axis_index("c"), dqkv, attn, keep_ref, give_ref)
    back_ref[:, width:] = attn
    for source, target in ((keep_ref, keep_hbm), (give_ref, give_hbm)):
        copies.append(pltpu.make_async_copy(source, target, sems.at[len(copies)]))
        copies[-1].start()
    dnormed = dot_nn(dqkv, w_qkv_ref[...]).astype(BF16).astype(F32)
    back_ref[:, :width] = norm_back(dnormed, normed, rate).astype(BF16)
    copies.append(pltpu.make_async_copy(back_ref, back_hbm, sems.at[4]))
    copies[-1].start()
    for copy in copies:
        copy.wait()


def start_all(copies):
    for copy in copies:
        copy.start()
    return copies


def load_all(pairs, sems, first=0):
    return start_all(
        [pltpu.make_async_copy(a, b, sems.at[first + place]) for place, (a, b) in enumerate(pairs)]
    )


def space_backward(
    cot_hbm, recv_hbm, w_out_hbm, qkv_hbm, attn_hbm, dhidden_hbm, dqkv_hbm, keep_ref, send_ref,
    cot_ref, dres_ref, w_out_ref, qkv_ref, attn_ref, dhidden_ref, dqkv_ref, sems,
):
    width = cot_ref.shape[1]
    loads = load_all(
        [
            (cot_hbm, cot_ref),
            (recv_hbm.at[:, pl.ds(0, width)], dres_ref),
            (w_out_hbm, w_out_ref),
            (qkv_hbm, qkv_ref),
            (attn_hbm, attn_ref),
        ],
        sems,
    )
    loads[0].wait()
    loads[1].wait()
    dhidden = cot_ref[...] + dres_ref[...]
    dhidden_ref[...] = dhidden
    stores = load_all([(dhidden_ref, dhidden_hbm)], sems, 5)
    loads[2].wait()
    dattn = dot_nt(dhidden, w_out_ref[...]).astype(BF16)
    loads[3].wait()
    query, keys, values = split_qkv(qkv_ref[...])
    dqkv = attention_back(query, keys, values, dattn, None, False)[1]
    dqkv_ref[...] = dqkv
    stores += load_all([(dqkv_ref, dqkv_hbm)], sems, 6)
    loads[4].wait()
    pair_up(lax.axis_index("c"), dqkv, attn_ref[...], keep_ref, send_ref)
    for store in stores:
        store.wait()


def space_finish(
    x_hbm, dhidden_hbm, dqkv_hbm, w_qkv_hbm, grad_ref, x_ref, dhidden_ref, dqkv_ref, w_qkv_ref, sems
):
    loads = load_all(
        [(x_hbm, x_ref), (dqkv_hbm, dqkv_ref), (w_qkv_hbm, w_qkv_ref), (dhidden_hbm, dhidden_ref)], sems
    )
    loads[0].wait()
    normed, rate = norm_parts(x_ref[...].astype(F32))
    loads[1].wait()
    loads[2].wait()
    dnormed = dot_nn(dqkv_ref[...], w_qkv_ref[...]).astype(BF16).astype(F32)
    dres = norm_back(dnormed, normed, rate).astype(BF16)
    loads[3].wait()
    grad_ref[...] = dhidden_ref[...] + dres


def call(kernel, outs, *args, flops=0, hbm_in=0, hbm_out=(), scratch=(), grant=8):
    size = sum(a.size * a.dtype.itemsize for a in args) + sum(math.prod(shape) * 2 for shape, _ in outs)
    vmem, hbm = pl.BlockSpec(memory_space=pltpu.VMEM), pl.BlockSpec(memory_space=pltpu.HBM)
    args = [
        pltpu.with_memory_space_constraint(arg, pltpu.HBM) if place < hbm_in else arg
        for place, arg in enumerate(args)
    ]
    return pl.pallas_call(
        kernel,
        out_shape=[
            pltpu.HBM(*out) if place in hbm_out else jax.ShapeDtypeStruct(*out)
            for place, out in enumerate(outs)
        ],
        in_specs=[hbm if place < hbm_in else vmem for place in range(len(args))],
        out_specs=[hbm if place in hbm_out else vmem for place in range(len(outs))],
        scratch_shapes=list(scratch),
        compiler_params=pltpu.CompilerParams(vmem_limit_bytes=grant * 1024 * 1024),
        cost_estimate=pl.CostEstimate(flops=flops // 1000, bytes_accessed=size // 1000, transcendentals=0),
    )(*args)


def chunk_rows(chunks, rows, part):
    table = np.zeros((3, chunks, 2, 8, chunks * rows), np.float32)
    for chunk in range(chunks):
        for lane in range(8):
            table[0, chunk, part, lane, chunk * rows + lane] = 1
            table[1, chunk, part, lane, chunk * rows + 8 + lane] = 1
        for lane in range(6):
            table[2, chunk, part, lane, chunk * rows + 16 + lane % 2] = 1
    return table.reshape(3 * chunks * 16, chunks * rows).astype(jnp.bfloat16)


def mix_out(
    x_hbm, attn_hbm, w_space_hbm, recv_hbm, w_time_hbm, mixed_ref,
    x_ref, attn_ref, w_space_ref, time_ref, w_time_ref, sems,
):
    width = x_ref.shape[1]
    loads = load_all(
        [
            (x_hbm, x_ref),
            (attn_hbm, attn_ref),
            (w_space_hbm, w_space_ref),
            (recv_hbm.at[:, pl.ds(width, HK)], time_ref),
            (w_time_hbm, w_time_ref),
        ],
        sems,
    )
    for load in loads:
        load.wait()
    hidden = (x_ref[...].astype(F32) + dot_nn(attn_ref[...], w_space_ref[...])).astype(BF16)
    mixed = hidden.astype(F32) + dot_nn(time_ref[...], w_time_ref[...])
    mixed_ref[...] = mixed.astype(BF16)


def pair_up(core, dqkv, attn, keep_ref, send_ref):
    second = jnp.concatenate([dqkv[:, 2 * HK :], attn], axis=1)
    first = dqkv[:, : 2 * HK]
    keep_ref[...] = jnp.where(core == 0, first, second)
    send_ref[...] = jnp.where(core == 0, second, first)


def weight_terms(lines, in_own, in_got, out_own, out_got, own_ref, got_ref, *refs):
    parts, total_ref = refs[:-1], refs[-1]
    width = own_ref.shape[1]
    low, high = HK // LANES * LANES, -(-HK // LANES) * LANES
    size = width // 3
    rows = width // (lines * lines)
    core = lax.axis_index("c")

    def product(one, two, left, right):
        return dot_tn(one, own_ref[:, left:right]) + dot_tn(two, got_ref[:, left:right])

    def place(me, order):
        for step, part_ref in enumerate(parts):
            line = lax.rem(me + step, lines)
            blocks = []
            for block in range(lines):
                start = pl.multiple_of(order(block, line) * rows, 8)
                blocks.append(total_ref[pl.ds(start, rows), :])
            part_ref[...] = jnp.concatenate(blocks, axis=0).astype(BF16)

    @pl.when(core == 0)
    def _():
        for start in range(0, width, size):
            block = slice(start, start + size)
            total_ref[block, :] = product(in_own[:, block], in_got[:, block], 0, width)
        place(lax.axis_index("z"), lambda block, line: line * lines + block)

    @pl.when(core != 0)
    def _():
        for start in range(0, width, size):
            block = slice(start, start + size)
            left = product(in_own[:, block], in_got[:, block], 0, high)
            right = product(out_own[:, block], out_got[:, block], low, width)
            lane = low + lax.broadcasted_iota(jnp.int32, (size, high - low), 1)
            total_ref[block, :low] = left[:, :low]
            total_ref[block, low:high] = jnp.where(lane < HK, left[:, low:], right[:, : high - low])
            total_ref[block, high:] = right[:, high - low :]
        place(lax.axis_index("y"), lambda block, line: block * lines + line)


def add_lines(table_ref, *refs):
    got, chunk_ref = refs[:4], refs[-1]
    width = got[0].shape[1]
    third = width // 3
    total = got[0][...].astype(F32)
    for ref in got[1:4]:
        total = total + ref[...].astype(F32)
    total = total.astype(BF16)
    block = table_ref.shape[0] // 3
    for part in range(3):
        whole = dot_nn(table_ref[part * block : (part + 1) * block, :], total)
        place = slice(part * width, min((part + 1) * width, 2 * width + third))
        if part == 2:
            row = lax.rem(lax.broadcasted_iota(jnp.int32, (block, third), 0), 8)
            whole = jnp.where(
                row < 2,
                whole[:, :third],
                jnp.where(row < 4, whole[:, third : 2 * third], whole[:, 2 * third :]),
            )
        whole = whole.astype(BF16)
        if len(refs) == 6:
            other = refs[4][:, place]
            row = lax.rem(lax.broadcasted_iota(jnp.int32, whole.shape, 0), 16)
            whole = jnp.where(row < 8, other, whole)
        chunk_ref[:, place] = whole


def add_chunks(scale, chunk_ref, keep_ref, send_ref):
    count, lanes = chunk_ref.shape
    total = chunk_ref[:16, :].astype(F32)
    for start in range(16, count, 16):
        total = total + chunk_ref[start : start + 16, :].astype(F32)
    total = total * scale
    width = lanes // 7 * 3
    third = width // 3
    core = lax.axis_index("c")
    for part in range(2):
        held = total[8 * part : 8 * part + 8]
        first, second, rest = held[:, :width], held[:, width : 2 * width], held[:, 2 * width :]
        last = jnp.concatenate([rest[0:2], rest[2:4], rest[4:6]], axis=1)
        low = jnp.concatenate([first, second[:1]], axis=0)
        high = jnp.concatenate([second[1:], last], axis=0)
        keep_ref[part] = jnp.where(core == 0, low, high)
        send_ref[part] = jnp.where(core == 0, high, low)


def place_rows(keep_ref, got_ref, qkv_time_ref, out_time_ref, qkv_space_ref, out_space_ref):
    core = lax.axis_index("c")
    for part, (qkv_ref, out_ref) in enumerate(
        ((qkv_time_ref, out_time_ref), (qkv_space_ref, out_space_ref))
    ):
        keep, got = keep_ref[part], got_ref[part]
        first = jnp.where(core == 0, keep, got)
        second = jnp.where(core == 0, got, keep)
        qkv_ref[:, : 2 * HK] = first
        qkv_ref[:, 2 * HK :] = second[:, :HK]
        out_ref[...] = second[:, HK:]


SEQ = ("z", "y", "xl")
ALL = ("z", "y", "xl", "xh", "c")
SIDE = 4


def device(z, y, x, core):
    return ((z * SIDE + y) * SIDE + x) * 2 + core


def line_pairs(step):
    pairs = []
    for z in range(SIDE):
        for y in range(SIDE):
            for x in range(SIDE):
                pairs.append((device(z, y, x, 0), device((z + step) % SIDE, y, x, 0)))
                pairs.append((device(z, y, x, 1), device(z, (y + step) % SIDE, x, 1)))
    return pairs


def plane_groups():
    side = range(SIDE)
    groups = [[device(z, y, x, 0) for y in side for x in side] for z in side]
    return groups + [[device(z, y, x, 1) for z in side for x in side] for y in side]


def on_device(clips, cotangent, w_qkv_space, w_out_space, w_qkv_time, w_out_time):
    patches, width = clips.shape[2], clips.shape[3]
    frames = lax.axis_size(SEQ)
    own_patches = patches // frames
    count = patches
    qkv_cols = w_qkv_space.shape[1]
    w_qkv_space, w_out_space = w_qkv_space.T, w_out_space.T
    w_qkv_time, w_out_time = w_qkv_time.T, w_out_time.T
    scale = 1.0 / math.sqrt(count * frames * lax.axis_size(("xh", "c")))
    x = clips.reshape(count, width)
    top = cotangent.reshape(count, width)
    plane = SIDE * SIDE
    rows = width // (plane * SIDE)
    tables = [jnp.asarray(chunk_rows(plane, rows, part)) for part in range(2)]
    half = ((count, width), BF16)
    quarter = ((width // SIDE, width), BF16)

    def swap(array):
        return lax.ppermute(array, "c", [(0, 1), (1, 0)])

    def exchange(array, axes, parts, groups=None):
        lanes = array.shape[1]
        array = lax.all_to_all(
            array.reshape(parts, -1, lanes),
            axes,
            split_axis=0,
            concat_axis=0,
            tiled=True,
            axis_index_groups=groups,
        )
        return array.reshape(-1, lanes)

    def terms(*args):
        return call(
            functools.partial(weight_terms, SIDE),
            [quarter] * SIDE,
            *args,
            flops=2 * 10**9,
            scratch=[pltpu.VMEM((width, width), F32)],
            grant=16,
        )

    def along_lines(parts):
        return [parts[0]] + [
            lax.ppermute(part, ALL, line_pairs(step)) for step, part in enumerate(parts) if step
        ]

    def buffers(*shapes):
        return [pltpu.VMEM(*shape) for shape in shapes]

    qkv = ((count, qkv_cols), BF16)
    mix = ((count, HK), BF16)
    send, qkv_space, attn_space, normed_space = call(
        space_forward,
        [((count, 2 * width), BF16), qkv, mix, half],
        x, top, w_qkv_space, w_out_space,
        flops=3 * 10**9,
        hbm_in=4,
        hbm_out=(1, 2, 3),
        scratch=buffers(half, ((qkv_cols, width), BF16), ((HK, width), BF16), qkv, mix, half)
        + [pltpu.SemaphoreType.DMA((9,))],
        grant=16,
    )
    recv = exchange(send, SEQ, frames)
    pack = ((count, width + HK), BF16)
    back, normed_time, top_time, keep, give = call(
        functools.partial(time_both, own_patches),
        [pack, half, half, half, half],
        recv, w_qkv_time, w_out_time,
        flops=5 * 10**9,
        hbm_out=(0, 1, 2, 3, 4),
        scratch=buffers(pack, half, half, half) + [pltpu.SemaphoreType.DMA((5,))],
        grant=16,
    )
    terms_time = terms(
        normed_time, swap(normed_time), top_time, swap(top_time), keep, swap(give)
    )
    recv = exchange(back, SEQ, frames)
    recv, terms_time = lax.optimization_barrier((recv, terms_time))
    got_time = along_lines(terms_time)
    wide = ((HK, width), BF16)
    dhidden, dqkv_space, keep, give = call(
        space_backward, [half, qkv, half, half],
        top, recv, w_out_space, qkv_space, attn_space,
        flops=3 * 10**9,
        hbm_in=5,
        hbm_out=(0, 1),
        scratch=buffers(half, half, wide, qkv, mix, half, qkv) + [pltpu.SemaphoreType.DMA((7,))],
        grant=20,
    )
    terms_space = terms(
        normed_space, swap(normed_space), dhidden, swap(dhidden), keep, swap(give)
    )
    got_space = along_lines(terms_space)
    grad_clips = call(
        space_finish, [half], x, dhidden, dqkv_space, w_qkv_space,
        flops=10**9,
        hbm_in=4,
        scratch=buffers(half, half, qkv, ((qkv_cols, width), BF16)) + [pltpu.SemaphoreType.DMA((4,))],
        grant=16,
    )[0]
    mixed = call(
        mix_out, [half], x, attn_space, w_out_space, recv, w_out_time,
        flops=10**9,
        hbm_in=5,
        scratch=buffers(half, mix, wide, mix, wide) + [pltpu.SemaphoreType.DMA((5,))],
        grant=16,
    )[0]
    chunk = [((plane * 16, 2 * width + width // 3), BF16)]
    chunks = call(add_lines, chunk, tables[0], *got_time, flops=10**9)[0]
    chunks = call(add_lines, chunk, tables[1], *got_space, chunks, flops=10**9)[0]
    chunks, grad_clips, mixed = lax.optimization_barrier((chunks, grad_clips, mixed))
    chunks = exchange(chunks, ALL, plane, plane_groups())
    own_rows = ((2, rows // 2, width), F32)
    own, other = call(functools.partial(add_chunks, scale), [own_rows, own_rows], chunks)
    grad_qkv = ((rows // 2, qkv_cols), F32)
    grad_out = ((rows // 2, HK), F32)
    grad_qkv_time, grad_out_time, grad_qkv_space, grad_out_space = call(
        place_rows, [grad_qkv, grad_out, grad_qkv, grad_out], own, swap(other)
    )
    return (
        mixed.reshape(clips.shape),
        grad_clips.reshape(clips.shape),
        grad_qkv_space,
        grad_out_space,
        grad_qkv_time,
        grad_out_time,
    )


def solution(mesh):
    fine = Mesh(mesh.devices.reshape(4, 4, 2, 2, 2), ("z", "y", "xl", "xh", "c"))
    tokens = P(("xh", "c"), SEQ, None, None)
    rows = P(("z", "y", "xl", "xh", "c"), None)
    return jax.shard_map(
        on_device,
        mesh=fine,
        in_specs=(tokens, tokens, P(), P(), P(), P()),
        out_specs=(tokens, tokens, rows, rows, rows, rows),
        check_vma=False,
    )
```

```python
import functools
import math

import jax
import jax.numpy as jnp
import numpy as np
from jax import lax
from jax.experimental import pallas as pl
from jax.experimental.pallas import tpu as pltpu
from jax.sharding import Mesh
from jax.sharding import PartitionSpec as P

HEADS = 8
HEAD_DIM = 72
HK = HEADS * HEAD_DIM
EPS = 1e-06
LANES = 128
F32 = jnp.float32
BF16 = jnp.bfloat16


def windows():
    out = []
    for head in range(HEADS):
        low, high = head * HEAD_DIM, (head + 1) * HEAD_DIM
        start = low // LANES * LANES
        stop = min(-(-high // LANES) * LANES, HK)
        out.append((low, high, start, stop))
    return out


def dot_nn(a, b):
    return lax.dot_general(a, b, (((1,), (0,)), ((), ())), preferred_element_type=F32)


def dot_nt(a, b):
    return lax.dot_general(a, b, (((1,), (1,)), ((), ())), preferred_element_type=F32)


def dot_tn(a, b):
    return lax.dot_general(a, b, (((0,), (0,)), ((), ())), preferred_element_type=F32)


def norm_parts(tokens):
    center = tokens - jnp.mean(tokens, axis=-1, keepdims=True)
    spread = jnp.mean(center * center, axis=-1, keepdims=True)
    rate = lax.rsqrt(spread + EPS)
    return center * rate, rate


def norm_back(grad, normed, rate):
    first = jnp.mean(grad, axis=-1, keepdims=True)
    second = jnp.mean(grad * normed, axis=-1, keepdims=True)
    return rate * (grad - first - normed * second)


def split_qkv(qkv):
    return qkv[:, :HK], qkv[:, HK : 2 * HK], qkv[:, 2 * HK :]


class HeadSum:
    def __init__(self):
        self.slabs = [None] * -(-HK // LANES)

    def put(self, head, piece):
        low, high, start, stop = windows()[head]
        for slab in range(start // LANES, -(-stop // LANES)):
            left, right = slab * LANES, min((slab + 1) * LANES, HK)
            part = piece[:, left - start : right - start]
            held = self.slabs[slab]
            if held is not None:
                lane = left + lax.broadcasted_iota(jnp.int32, part.shape, 1)
                part = jnp.where((lane >= low) & (lane < high), part, held)
            self.slabs[slab] = part

    def whole(self, dtype):
        return jnp.concatenate([slab.astype(dtype) for slab in self.slabs], axis=1)


def head_part(array, head):
    low, high, start, stop = windows()[head]
    part = array[:, start:stop]
    lane = start + lax.broadcasted_iota(jnp.int32, part.shape, 1)
    return jnp.where((lane >= low) & (lane < high), part, jnp.zeros_like(part))


def head_window(array, head):
    _, _, start, stop = windows()[head]
    return array[:, start:stop]


def soft_t(scores, keep):
    if keep is not None:
        scores = jnp.where(keep, scores, -1e30)
    peak = jnp.max(scores, axis=0, keepdims=True)
    weights = jnp.exp2((scores - peak) * (HEAD_DIM ** (-0.5) * math.log2(math.e)))
    return weights * (1.0 / jnp.sum(weights, axis=0, keepdims=True))


def score_t(query, keys, head):
    return dot_nt(head_part(keys, head), head_window(query, head))


def same_patch(count, patches):
    row = lax.broadcasted_iota(jnp.int32, (count, count), 0)
    col = lax.broadcasted_iota(jnp.int32, (count, count), 1)
    return lax.rem(row, patches) == lax.rem(col, patches)


def space_forward(
    x_hbm, cot_hbm, w_qkv_hbm, w_out_hbm, send_ref, qkv_hbm, attn_hbm, normed_hbm,
    x_ref, w_qkv_ref, w_out_ref, qkv_ref, attn_ref, normed_ref, sems,
):
    width = x_ref.shape[1]
    load_x = pltpu.make_async_copy(x_hbm, x_ref, sems.at[0])
    load_x.start()
    loads = []
    for part in range(3):
        rows = pl.ds(part * HK, HK)
        loads.append(pltpu.make_async_copy(w_qkv_hbm.at[rows, :], w_qkv_ref.at[rows, :], sems.at[1 + part]))
    load_out = pltpu.make_async_copy(w_out_hbm, w_out_ref, sems.at[4])
    load_cot = pltpu.make_async_copy(cot_hbm, send_ref.at[:, pl.ds(width, width)], sems.at[5])
    for load in loads + [load_out, load_cot]:
        load.start()
    load_x.wait()
    x = x_ref[...].astype(F32)
    normed = norm_parts(x)[0].astype(BF16)
    normed_ref[...] = normed
    store_normed = pltpu.make_async_copy(normed_ref, normed_hbm, sems.at[6])
    store_normed.start()
    parts = []
    for part, load in enumerate(loads):
        load.wait()
        parts.append(dot_nt(normed, w_qkv_ref[part * HK : (part + 1) * HK, :]).astype(BF16))
    query, keys, values = parts
    qkv_ref[...] = jnp.concatenate(parts, axis=1)
    store_qkv = pltpu.make_async_copy(qkv_ref, qkv_hbm, sems.at[7])
    store_qkv.start()
    mix = HeadSum()
    for heads in (range(HEADS),):
        scores = [score_t(query, keys, head) for head in heads]
        weights = [soft_t(score, None).astype(BF16) for score in scores]
        for head, weight in zip(heads, weights):
            mix.put(head, dot_tn(weight, head_window(values, head)))
    attn = mix.whole(BF16)
    attn_ref[...] = attn
    store_attn = pltpu.make_async_copy(attn_ref, attn_hbm, sems.at[8])
    store_attn.start()
    load_out.wait()
    send_ref[:, :width] = (x + dot_nn(attn, w_out_ref[...])).astype(BF16)
    for copy in (load_cot, store_normed, store_qkv, store_attn):
        copy.wait()


def attention_back(query, keys, values, dmix, keep, forward):
    mix, dq, dk, dv = HeadSum(), HeadSum(), HeadSum(), HeadSum()
    for heads in (range(HEADS),):
        scores = [score_t(query, keys, head) for head in heads]
        dprobs = [dot_nt(head_part(values, head), head_window(dmix, head)).astype(BF16) for head in heads]
        weights = [soft_t(score, keep) for score in scores]
        rounded = [weight.astype(BF16) for weight in weights]
        dscores = []
        for weight, dprob in zip(weights, dprobs):
            dprob = dprob.astype(F32)
            total = jnp.sum(weight * dprob, axis=0, keepdims=True)
            dscores.append((weight * (dprob - total) * HEAD_DIM ** (-0.5)).astype(BF16))
        for place, head in enumerate(heads):
            if forward:
                mix.put(head, dot_tn(rounded[place], head_window(values, head)))
            dv.put(head, dot_nn(rounded[place], head_window(dmix, head)))
            dk.put(head, dot_nn(dscores[place], head_window(query, head)))
            dq.put(head, dot_tn(dscores[place], head_window(keys, head)))
    dqkv = jnp.concatenate([dq.whole(BF16), dk.whole(BF16), dv.whole(BF16)], axis=1)
    return (mix.whole(BF16) if forward else None), dqkv


def time_both(
    patches, recv_ref, w_qkv_ref, w_out_ref, back_hbm, normed_hbm, top_hbm, keep_hbm, give_hbm,
    back_ref, normed_ref, keep_ref, give_ref, sems,
):
    width = w_qkv_ref.shape[1]
    hidden = recv_ref[:, :width].astype(F32)
    normed, rate = norm_parts(hidden)
    rounded = normed.astype(BF16)
    normed_ref[...] = rounded
    copies = [
        pltpu.make_async_copy(normed_ref, normed_hbm, sems.at[0]),
        pltpu.make_async_copy(recv_ref.at[:, pl.ds(width, width)], top_hbm, sems.at[1]),
    ]
    for copy in copies:
        copy.start()
    qkv = dot_nt(rounded, w_qkv_ref[...]).astype(BF16)
    dattn = dot_nt(recv_ref[:, width:], w_out_ref[...]).astype(BF16)
    query, keys, values = split_qkv(qkv)
    keep = same_patch(hidden.shape[0], patches)
    attn, dqkv = attention_back(query, keys, values, dattn, keep, True)
    pair_up(lax.axis_index("c"), dqkv, attn, keep_ref, give_ref)
    back_ref[:, width:] = attn
    for source, target in ((keep_ref, keep_hbm), (give_ref, give_hbm)):
        copies.append(pltpu.make_async_copy(source, target, sems.at[len(copies)]))
        copies[-1].start()
    dnormed = dot_nn(dqkv, w_qkv_ref[...]).astype(BF16).astype(F32)
    back_ref[:, :width] = norm_back(dnormed, normed, rate).astype(BF16)
    copies.append(pltpu.make_async_copy(back_ref, back_hbm, sems.at[4]))
    copies[-1].start()
    for copy in copies:
        copy.wait()


def start_all(copies):
    for copy in copies:
        copy.start()
    return copies


def load_all(pairs, sems, first=0):
    return start_all(
        [pltpu.make_async_copy(a, b, sems.at[first + place]) for place, (a, b) in enumerate(pairs)]
    )


def space_backward(
    cot_hbm, recv_hbm, w_out_hbm, qkv_hbm, attn_hbm, normed_hbm,
    dhidden_ref, dqkv_ref, keep_ref, send_ref, normed_ref,
    cot_ref, dres_ref, w_out_ref, qkv_ref, attn_ref, sems,
):
    width = cot_ref.shape[1]
    loads = load_all(
        [
            (cot_hbm, cot_ref),
            (recv_hbm.at[:, pl.ds(0, width)], dres_ref),
            (w_out_hbm, w_out_ref),
            (qkv_hbm, qkv_ref),
            (attn_hbm, attn_ref),
            (normed_hbm, normed_ref),
        ],
        sems,
    )
    loads[0].wait()
    loads[1].wait()
    dhidden = cot_ref[...] + dres_ref[...]
    dhidden_ref[...] = dhidden
    loads[2].wait()
    dattn = dot_nt(dhidden, w_out_ref[...]).astype(BF16)
    loads[3].wait()
    query, keys, values = split_qkv(qkv_ref[...])
    dqkv = attention_back(query, keys, values, dattn, None, False)[1]
    dqkv_ref[...] = dqkv
    loads[4].wait()
    pair_up(lax.axis_index("c"), dqkv, attn_ref[...], keep_ref, send_ref)
    loads[5].wait()


def space_finish(x_hbm, w_qkv_hbm, dhidden_ref, dqkv_ref, grad_ref, x_ref, w_qkv_ref, sems):
    loads = load_all([(x_hbm, x_ref), (w_qkv_hbm, w_qkv_ref)], sems)
    loads[0].wait()
    normed, rate = norm_parts(x_ref[...].astype(F32))
    loads[1].wait()
    dnormed = dot_nn(dqkv_ref[...], w_qkv_ref[...]).astype(BF16).astype(F32)
    dres = norm_back(dnormed, normed, rate).astype(BF16)
    grad_ref[...] = dhidden_ref[...] + dres


def call(kernel, outs, *args, flops=0, hbm_in=0, hbm_out=(), scratch=(), grant=8):
    size = sum(a.size * a.dtype.itemsize for a in args) + sum(math.prod(shape) * 2 for shape, _ in outs)
    vmem, hbm = pl.BlockSpec(memory_space=pltpu.VMEM), pl.BlockSpec(memory_space=pltpu.HBM)
    args = [
        pltpu.with_memory_space_constraint(arg, pltpu.HBM) if place < hbm_in else arg
        for place, arg in enumerate(args)
    ]
    return pl.pallas_call(
        kernel,
        out_shape=[
            pltpu.HBM(*out) if place in hbm_out else jax.ShapeDtypeStruct(*out)
            for place, out in enumerate(outs)
        ],
        in_specs=[hbm if place < hbm_in else vmem for place in range(len(args))],
        out_specs=[hbm if place in hbm_out else vmem for place in range(len(outs))],
        scratch_shapes=list(scratch),
        compiler_params=pltpu.CompilerParams(vmem_limit_bytes=grant * 1024 * 1024),
        cost_estimate=pl.CostEstimate(flops=flops // 1000, bytes_accessed=size // 1000, transcendentals=0),
    )(*args)


def chunk_rows(chunks, rows, part):
    table = np.zeros((3, chunks, 2, 8, chunks * rows), np.float32)
    for chunk in range(chunks):
        for lane in range(8):
            table[0, chunk, part, lane, chunk * rows + lane] = 1
            table[1, chunk, part, lane, chunk * rows + 8 + lane] = 1
        for lane in range(6):
            table[2, chunk, part, lane, chunk * rows + 16 + lane % 2] = 1
    return table.reshape(3 * chunks * 16, chunks * rows).astype(jnp.bfloat16)


def mix_out(
    x_hbm, attn_hbm, w_space_hbm, recv_hbm, w_time_hbm, mixed_ref,
    x_ref, attn_ref, w_space_ref, time_ref, w_time_ref, sems,
):
    width = x_ref.shape[1]
    loads = load_all(
        [
            (x_hbm, x_ref),
            (attn_hbm, attn_ref),
            (w_space_hbm, w_space_ref),
            (recv_hbm.at[:, pl.ds(width, HK)], time_ref),
            (w_time_hbm, w_time_ref),
        ],
        sems,
    )
    for load in loads:
        load.wait()
    hidden = (x_ref[...].astype(F32) + dot_nn(attn_ref[...], w_space_ref[...])).astype(BF16)
    mixed = hidden.astype(F32) + dot_nn(time_ref[...], w_time_ref[...])
    mixed_ref[...] = mixed.astype(BF16)


def pair_up(core, dqkv, attn, keep_ref, send_ref):
    second = jnp.concatenate([dqkv[:, 2 * HK :], attn], axis=1)
    first = dqkv[:, : 2 * HK]
    keep_ref[...] = jnp.where(core == 0, first, second)
    send_ref[...] = jnp.where(core == 0, second, first)


def weight_terms(lines, in_own, in_got, out_own, out_got, own_ref, got_ref, *refs):
    parts, total_ref = refs[:-1], refs[-1]
    width = own_ref.shape[1]
    low, high = HK // LANES * LANES, -(-HK // LANES) * LANES
    size = width // 3
    rows = width // (lines * lines)
    core = lax.axis_index("c")

    def product(one, two, left, right):
        return dot_tn(one, own_ref[:, left:right]) + dot_tn(two, got_ref[:, left:right])

    def place(me, order):
        for step, part_ref in enumerate(parts):
            line = lax.rem(me + step, lines)
            blocks = []
            for block in range(lines):
                start = pl.multiple_of(order(block, line) * rows, 8)
                blocks.append(total_ref[pl.ds(start, rows), :])
            part_ref[...] = jnp.concatenate(blocks, axis=0).astype(BF16)

    @pl.when(core == 0)
    def _():
        for start in range(0, width, size):
            block = slice(start, start + size)
            total_ref[block, :] = product(in_own[:, block], in_got[:, block], 0, width)
        place(lax.axis_index("z"), lambda block, line: line * lines + block)

    @pl.when(core != 0)
    def _():
        for start in range(0, width, size):
            block = slice(start, start + size)
            left = product(in_own[:, block], in_got[:, block], 0, high)
            right = product(out_own[:, block], out_got[:, block], low, width)
            lane = low + lax.broadcasted_iota(jnp.int32, (size, high - low), 1)
            total_ref[block, :low] = left[:, :low]
            total_ref[block, low:high] = jnp.where(lane < HK, left[:, low:], right[:, : high - low])
            total_ref[block, high:] = right[:, high - low :]
        place(lax.axis_index("y"), lambda block, line: block * lines + line)


def add_lines(table_ref, *refs):
    got, chunk_ref = refs[:4], refs[-1]
    width = got[0].shape[1]
    third = width // 3
    total = got[0][...].astype(F32)
    for ref in got[1:4]:
        total = total + ref[...].astype(F32)
    total = total.astype(BF16)
    block = table_ref.shape[0] // 3
    for part in range(3):
        whole = dot_nn(table_ref[part * block : (part + 1) * block, :], total)
        place = slice(part * width, min((part + 1) * width, 2 * width + third))
        if part == 2:
            row = lax.rem(lax.broadcasted_iota(jnp.int32, (block, third), 0), 8)
            whole = jnp.where(
                row < 2,
                whole[:, :third],
                jnp.where(row < 4, whole[:, third : 2 * third], whole[:, 2 * third :]),
            )
        whole = whole.astype(BF16)
        if len(refs) == 6:
            other = refs[4][:, place]
            row = lax.rem(lax.broadcasted_iota(jnp.int32, whole.shape, 0), 16)
            whole = jnp.where(row < 8, other, whole)
        chunk_ref[:, place] = whole


def add_chunks(scale, chunk_ref, keep_ref, send_ref):
    count, lanes = chunk_ref.shape
    total = chunk_ref[:16, :].astype(F32)
    for start in range(16, count, 16):
        total = total + chunk_ref[start : start + 16, :].astype(F32)
    total = total * scale
    width = lanes // 7 * 3
    third = width // 3
    core = lax.axis_index("c")
    for part in range(2):
        held = total[8 * part : 8 * part + 8]
        first, second, rest = held[:, :width], held[:, width : 2 * width], held[:, 2 * width :]
        last = jnp.concatenate([rest[0:2], rest[2:4], rest[4:6]], axis=1)
        low = jnp.concatenate([first, second[:1]], axis=0)
        high = jnp.concatenate([second[1:], last], axis=0)
        keep_ref[part] = jnp.where(core == 0, low, high)
        send_ref[part] = jnp.where(core == 0, high, low)


def place_rows(keep_ref, got_ref, qkv_time_ref, out_time_ref, qkv_space_ref, out_space_ref):
    core = lax.axis_index("c")
    for part, (qkv_ref, out_ref) in enumerate(
        ((qkv_time_ref, out_time_ref), (qkv_space_ref, out_space_ref))
    ):
        keep, got = keep_ref[part], got_ref[part]
        first = jnp.where(core == 0, keep, got)
        second = jnp.where(core == 0, got, keep)
        qkv_ref[:, : 2 * HK] = first
        qkv_ref[:, 2 * HK :] = second[:, :HK]
        out_ref[...] = second[:, HK:]


SEQ = ("z", "y", "xl")
ALL = ("z", "y", "xl", "xh", "c")
SIDE = 4


def device(z, y, x, core):
    return ((z * SIDE + y) * SIDE + x) * 2 + core


def line_pairs(step):
    pairs = []
    for z in range(SIDE):
        for y in range(SIDE):
            for x in range(SIDE):
                pairs.append((device(z, y, x, 0), device((z + step) % SIDE, y, x, 0)))
                pairs.append((device(z, y, x, 1), device(z, (y + step) % SIDE, x, 1)))
    return pairs


def plane_groups():
    side = range(SIDE)
    groups = [[device(z, y, x, 0) for y in side for x in side] for z in side]
    return groups + [[device(z, y, x, 1) for z in side for x in side] for y in side]


def on_device(clips, cotangent, w_qkv_space, w_out_space, w_qkv_time, w_out_time):
    patches, width = clips.shape[2], clips.shape[3]
    frames = lax.axis_size(SEQ)
    own_patches = patches // frames
    count = patches
    qkv_cols = w_qkv_space.shape[1]
    w_qkv_space, w_out_space = w_qkv_space.T, w_out_space.T
    w_qkv_time, w_out_time = w_qkv_time.T, w_out_time.T
    scale = 1.0 / math.sqrt(count * frames * lax.axis_size(("xh", "c")))
    x = clips.reshape(count, width)
    top = cotangent.reshape(count, width)
    plane = SIDE * SIDE
    rows = width // (plane * SIDE)
    tables = [jnp.asarray(chunk_rows(plane, rows, part)) for part in range(2)]
    half = ((count, width), BF16)
    quarter = ((width // SIDE, width), BF16)

    def swap(array):
        return lax.ppermute(array, "c", [(0, 1), (1, 0)])

    def exchange(array, axes, parts, groups=None):
        lanes = array.shape[1]
        array = lax.all_to_all(
            array.reshape(parts, -1, lanes),
            axes,
            split_axis=0,
            concat_axis=0,
            tiled=True,
            axis_index_groups=groups,
        )
        return array.reshape(-1, lanes)

    def terms(*args):
        return call(
            functools.partial(weight_terms, SIDE),
            [quarter] * SIDE,
            *args,
            flops=2 * 10**9,
            scratch=[pltpu.VMEM((width, width), F32)],
            grant=16,
        )

    def along_lines(parts):
        return [parts[0]] + [
            lax.ppermute(part, ALL, line_pairs(step)) for step, part in enumerate(parts) if step
        ]

    def buffers(*shapes):
        return [pltpu.VMEM(*shape) for shape in shapes]

    qkv = ((count, qkv_cols), BF16)
    mix = ((count, HK), BF16)
    send, qkv_space, attn_space, normed_space = call(
        space_forward,
        [((count, 2 * width), BF16), qkv, mix, half],
        x, top, w_qkv_space, w_out_space,
        flops=3 * 10**9,
        hbm_in=4,
        hbm_out=(1, 2, 3),
        scratch=buffers(half, ((qkv_cols, width), BF16), ((HK, width), BF16), qkv, mix, half)
        + [pltpu.SemaphoreType.DMA((9,))],
        grant=16,
    )
    recv = exchange(send, SEQ, frames)
    pack = ((count, width + HK), BF16)
    back, normed_time, top_time, keep, give = call(
        functools.partial(time_both, own_patches),
        [pack, half, half, half, half],
        recv, w_qkv_time, w_out_time,
        flops=5 * 10**9,
        hbm_out=(0, 1, 2, 3, 4),
        scratch=buffers(pack, half, half, half) + [pltpu.SemaphoreType.DMA((5,))],
        grant=16,
    )
    terms_time = terms(
        normed_time, swap(normed_time), top_time, swap(top_time), keep, swap(give)
    )
    recv = exchange(back, SEQ, frames)
    recv, terms_time = lax.optimization_barrier((recv, terms_time))
    got_time = along_lines(terms_time)
    wide = ((HK, width), BF16)
    dhidden, dqkv_space, keep, give, normed_space = call(
        space_backward, [half, qkv, half, half, half],
        top, recv, w_out_space, qkv_space, attn_space, normed_space,
        flops=3 * 10**9,
        hbm_in=6,
        scratch=buffers(half, half, wide, qkv, mix) + [pltpu.SemaphoreType.DMA((6,))],
        grant=20,
    )
    keep, got_time[1], got_time[3] = lax.optimization_barrier((keep, got_time[1], got_time[3]))
    terms_space = terms(
        normed_space, swap(normed_space), dhidden, swap(dhidden), keep, swap(give)
    )
    got_space = along_lines(terms_space)
    grad_clips = call(
        space_finish, [half], x, w_qkv_space, dhidden, dqkv_space,
        flops=10**9,
        hbm_in=2,
        scratch=buffers(half, ((qkv_cols, width), BF16)) + [pltpu.SemaphoreType.DMA((2,))],
        grant=16,
    )[0]
    mixed = call(
        mix_out, [half], x, attn_space, w_out_space, recv, w_out_time,
        flops=10**9,
        hbm_in=5,
        scratch=buffers(half, mix, wide, mix, wide) + [pltpu.SemaphoreType.DMA((5,))],
        grant=16,
    )[0]
    chunk = [((plane * 16, 2 * width + width // 3), BF16)]
    chunks = call(add_lines, chunk, tables[0], *got_time, flops=10**9)[0]
    chunks = call(add_lines, chunk, tables[1], *got_space, chunks, flops=10**9)[0]
    chunks, grad_clips, mixed = lax.optimization_barrier((chunks, grad_clips, mixed))
    chunks = exchange(chunks, ALL, plane, plane_groups())
    own_rows = ((2, rows // 2, width), F32)
    own, other = call(functools.partial(add_chunks, scale), [own_rows, own_rows], chunks)
    grad_qkv = ((rows // 2, qkv_cols), F32)
    grad_out = ((rows // 2, HK), F32)
    grad_qkv_time, grad_out_time, grad_qkv_space, grad_out_space = call(
        place_rows, [grad_qkv, grad_out, grad_qkv, grad_out], own, swap(other)
    )
    return (
        mixed.reshape(clips.shape),
        grad_clips.reshape(clips.shape),
        grad_qkv_space,
        grad_out_space,
        grad_qkv_time,
        grad_out_time,
    )


def solution(mesh):
    fine = Mesh(mesh.devices.reshape(4, 4, 2, 2, 2), ("z", "y", "xl", "xh", "c"))
    tokens = P(("xh", "c"), SEQ, None, None)
    rows = P(("z", "y", "xl", "xh", "c"), None)
    return jax.shard_map(
        on_device,
        mesh=fine,
        in_specs=(tokens, tokens, P(), P(), P(), P()),
        out_specs=(tokens, tokens, rows, rows, rows, rows),
        check_vma=False,
    )
```

```python
import functools
import math

import jax
import jax.numpy as jnp
import numpy as np
from jax import lax
from jax.experimental import pallas as pl
from jax.experimental.pallas import tpu as pltpu
from jax.sharding import Mesh
from jax.sharding import PartitionSpec as P

HEADS = 8
HEAD_DIM = 72
HK = HEADS * HEAD_DIM
EPS = 1e-06
LANES = 128
F32 = jnp.float32
BF16 = jnp.bfloat16


def windows():
    out = []
    for head in range(HEADS):
        low, high = head * HEAD_DIM, (head + 1) * HEAD_DIM
        start = low // LANES * LANES
        stop = min(-(-high // LANES) * LANES, HK)
        out.append((low, high, start, stop))
    return out


def dot_nn(a, b):
    return lax.dot_general(a, b, (((1,), (0,)), ((), ())), preferred_element_type=F32)


def dot_nt(a, b):
    return lax.dot_general(a, b, (((1,), (1,)), ((), ())), preferred_element_type=F32)


def dot_tn(a, b):
    return lax.dot_general(a, b, (((0,), (0,)), ((), ())), preferred_element_type=F32)


def norm_parts(tokens):
    center = tokens - jnp.mean(tokens, axis=-1, keepdims=True)
    spread = jnp.mean(center * center, axis=-1, keepdims=True)
    rate = lax.rsqrt(spread + EPS)
    return center * rate, rate


def norm_back(grad, normed, rate):
    first = jnp.mean(grad, axis=-1, keepdims=True)
    second = jnp.mean(grad * normed, axis=-1, keepdims=True)
    return rate * (grad - first - normed * second)


def split_qkv(qkv):
    return qkv[:, :HK], qkv[:, HK : 2 * HK], qkv[:, 2 * HK :]


class HeadSum:
    def __init__(self):
        self.slabs = [None] * -(-HK // LANES)

    def put(self, head, piece):
        low, high, start, stop = windows()[head]
        for slab in range(start // LANES, -(-stop // LANES)):
            left, right = slab * LANES, min((slab + 1) * LANES, HK)
            part = piece[:, left - start : right - start]
            held = self.slabs[slab]
            if held is not None:
                lane = left + lax.broadcasted_iota(jnp.int32, part.shape, 1)
                part = jnp.where((lane >= low) & (lane < high), part, held)
            self.slabs[slab] = part

    def whole(self, dtype):
        return jnp.concatenate([slab.astype(dtype) for slab in self.slabs], axis=1)


def head_part(array, head):
    low, high, start, stop = windows()[head]
    part = array[:, start:stop]
    lane = start + lax.broadcasted_iota(jnp.int32, part.shape, 1)
    return jnp.where((lane >= low) & (lane < high), part, jnp.zeros_like(part))


def head_window(array, head):
    _, _, start, stop = windows()[head]
    return array[:, start:stop]


def soft_t(scores, keep):
    if keep is not None:
        scores = jnp.where(keep, scores, -1e30)
    peak = jnp.max(scores, axis=0, keepdims=True)
    weights = jnp.exp2((scores - peak) * (HEAD_DIM ** (-0.5) * math.log2(math.e)))
    return weights * (1.0 / jnp.sum(weights, axis=0, keepdims=True))


def score_t(query, keys, head):
    return dot_nt(head_part(keys, head), head_window(query, head))


def same_patch(count, patches):
    row = lax.broadcasted_iota(jnp.int32, (count, count), 0)
    col = lax.broadcasted_iota(jnp.int32, (count, count), 1)
    return lax.rem(row, patches) == lax.rem(col, patches)


def space_forward(
    x_hbm, cot_hbm, w_qkv_hbm, w_out_hbm, send_ref, qkv_hbm, attn_hbm, normed_hbm,
    x_ref, w_qkv_ref, w_out_ref, qkv_ref, attn_ref, normed_ref, sems,
):
    width = x_ref.shape[1]
    load_x = pltpu.make_async_copy(x_hbm, x_ref, sems.at[0])
    load_x.start()
    loads = []
    for part in range(3):
        rows = pl.ds(part * HK, HK)
        loads.append(pltpu.make_async_copy(w_qkv_hbm.at[rows, :], w_qkv_ref.at[rows, :], sems.at[1 + part]))
    load_out = pltpu.make_async_copy(w_out_hbm, w_out_ref, sems.at[4])
    load_cot = pltpu.make_async_copy(cot_hbm, send_ref.at[:, pl.ds(width, width)], sems.at[5])
    for load in loads + [load_out, load_cot]:
        load.start()
    load_x.wait()
    x = x_ref[...].astype(F32)
    normed = norm_parts(x)[0].astype(BF16)
    normed_ref[...] = normed
    store_normed = pltpu.make_async_copy(normed_ref, normed_hbm, sems.at[6])
    store_normed.start()
    parts = []
    for part, load in enumerate(loads):
        load.wait()
        parts.append(dot_nt(normed, w_qkv_ref[part * HK : (part + 1) * HK, :]).astype(BF16))
    query, keys, values = parts
    qkv_ref[...] = jnp.concatenate(parts, axis=1)
    store_qkv = pltpu.make_async_copy(qkv_ref, qkv_hbm, sems.at[7])
    store_qkv.start()
    mix = HeadSum()
    for heads in (range(HEADS),):
        scores = [score_t(query, keys, head) for head in heads]
        weights = [soft_t(score, None).astype(BF16) for score in scores]
        for head, weight in zip(heads, weights):
            mix.put(head, dot_tn(weight, head_window(values, head)))
    attn = mix.whole(BF16)
    attn_ref[...] = attn
    store_attn = pltpu.make_async_copy(attn_ref, attn_hbm, sems.at[8])
    store_attn.start()
    load_out.wait()
    send_ref[:, :width] = (x + dot_nn(attn, w_out_ref[...])).astype(BF16)
    for copy in (load_cot, store_normed, store_qkv, store_attn):
        copy.wait()


def attention_back(query, keys, values, dmix, keep, forward):
    mix, dq, dk, dv = HeadSum(), HeadSum(), HeadSum(), HeadSum()
    for heads in (range(HEADS),):
        scores = [score_t(query, keys, head) for head in heads]
        dprobs = [dot_nt(head_part(values, head), head_window(dmix, head)).astype(BF16) for head in heads]
        weights = [soft_t(score, keep) for score in scores]
        rounded = [weight.astype(BF16) for weight in weights]
        dscores = []
        for weight, dprob in zip(weights, dprobs):
            dprob = dprob.astype(F32)
            total = jnp.sum(weight * dprob, axis=0, keepdims=True)
            dscores.append((weight * (dprob - total) * HEAD_DIM ** (-0.5)).astype(BF16))
        for place, head in enumerate(heads):
            if forward:
                mix.put(head, dot_tn(rounded[place], head_window(values, head)))
            dv.put(head, dot_nn(rounded[place], head_window(dmix, head)))
            dk.put(head, dot_nn(dscores[place], head_window(query, head)))
            dq.put(head, dot_tn(dscores[place], head_window(keys, head)))
    dqkv = jnp.concatenate([dq.whole(BF16), dk.whole(BF16), dv.whole(BF16)], axis=1)
    return (mix.whole(BF16) if forward else None), dqkv


def time_both(
    patches, recv_ref, w_qkv_ref, w_out_ref, back_hbm, normed_hbm, top_hbm, keep_hbm, give_hbm,
    back_ref, normed_ref, keep_ref, give_ref, sems,
):
    width = w_qkv_ref.shape[1]
    hidden = recv_ref[:, :width].astype(F32)
    normed, rate = norm_parts(hidden)
    rounded = normed.astype(BF16)
    normed_ref[...] = rounded
    copies = [
        pltpu.make_async_copy(normed_ref, normed_hbm, sems.at[0]),
        pltpu.make_async_copy(recv_ref.at[:, pl.ds(width, width)], top_hbm, sems.at[1]),
    ]
    for copy in copies:
        copy.start()
    qkv = dot_nt(rounded, w_qkv_ref[...]).astype(BF16)
    dattn = dot_nt(recv_ref[:, width:], w_out_ref[...]).astype(BF16)
    query, keys, values = split_qkv(qkv)
    keep = same_patch(hidden.shape[0], patches)
    attn, dqkv = attention_back(query, keys, values, dattn, keep, True)
    pair_up(lax.axis_index("c"), dqkv, attn, keep_ref, give_ref)
    back_ref[:, width:] = attn
    for source, target in ((keep_ref, keep_hbm), (give_ref, give_hbm)):
        copies.append(pltpu.make_async_copy(source, target, sems.at[len(copies)]))
        copies[-1].start()
    count = back_ref.shape[0]
    for start in range(0, count, count // 2):
        block = slice(start, start + count // 2)
        dnormed = dot_nn(dqkv[block], w_qkv_ref[...]).astype(BF16).astype(F32)
        back_ref[block, :width] = norm_back(dnormed, normed[block], rate[block]).astype(BF16)
        rows = pl.ds(start, count // 2)
        copies.append(
            pltpu.make_async_copy(back_ref.at[rows, :], back_hbm.at[rows, :], sems.at[len(copies)])
        )
        copies[-1].start()
    for copy in copies:
        copy.wait()


def start_all(copies):
    for copy in copies:
        copy.start()
    return copies


def load_all(pairs, sems, first=0):
    return start_all(
        [pltpu.make_async_copy(a, b, sems.at[first + place]) for place, (a, b) in enumerate(pairs)]
    )


def space_backward(
    cot_hbm, recv_hbm, w_out_hbm, qkv_hbm, attn_hbm, normed_hbm,
    dhidden_ref, dqkv_ref, keep_ref, send_ref, normed_ref,
    cot_ref, dres_ref, w_out_ref, qkv_ref, attn_ref, sems,
):
    width = cot_ref.shape[1]
    loads = load_all(
        [
            (cot_hbm, cot_ref),
            (recv_hbm.at[:, pl.ds(0, width)], dres_ref),
            (w_out_hbm, w_out_ref),
            (qkv_hbm, qkv_ref),
            (attn_hbm, attn_ref),
            (normed_hbm, normed_ref),
        ],
        sems,
    )
    loads[0].wait()
    loads[1].wait()
    dhidden = cot_ref[...] + dres_ref[...]
    dhidden_ref[...] = dhidden
    loads[2].wait()
    dattn = dot_nt(dhidden, w_out_ref[...]).astype(BF16)
    loads[3].wait()
    query, keys, values = split_qkv(qkv_ref[...])
    dqkv = attention_back(query, keys, values, dattn, None, False)[1]
    dqkv_ref[...] = dqkv
    loads[4].wait()
    pair_up(lax.axis_index("c"), dqkv, attn_ref[...], keep_ref, send_ref)
    loads[5].wait()


def space_finish(x_hbm, w_qkv_hbm, dhidden_ref, dqkv_ref, grad_ref, x_ref, w_qkv_ref, sems):
    loads = load_all([(x_hbm, x_ref), (w_qkv_hbm, w_qkv_ref)], sems)
    loads[0].wait()
    normed, rate = norm_parts(x_ref[...].astype(F32))
    loads[1].wait()
    dnormed = dot_nn(dqkv_ref[...], w_qkv_ref[...]).astype(BF16).astype(F32)
    dres = norm_back(dnormed, normed, rate).astype(BF16)
    grad_ref[...] = dhidden_ref[...] + dres


def call(kernel, outs, *args, flops=0, hbm_in=0, hbm_out=(), scratch=(), grant=8):
    size = sum(a.size * a.dtype.itemsize for a in args) + sum(math.prod(shape) * 2 for shape, _ in outs)
    vmem, hbm = pl.BlockSpec(memory_space=pltpu.VMEM), pl.BlockSpec(memory_space=pltpu.HBM)
    args = [
        pltpu.with_memory_space_constraint(arg, pltpu.HBM) if place < hbm_in else arg
        for place, arg in enumerate(args)
    ]
    return pl.pallas_call(
        kernel,
        out_shape=[
            pltpu.HBM(*out) if place in hbm_out else jax.ShapeDtypeStruct(*out)
            for place, out in enumerate(outs)
        ],
        in_specs=[hbm if place < hbm_in else vmem for place in range(len(args))],
        out_specs=[hbm if place in hbm_out else vmem for place in range(len(outs))],
        scratch_shapes=list(scratch),
        compiler_params=pltpu.CompilerParams(vmem_limit_bytes=grant * 1024 * 1024),
        cost_estimate=pl.CostEstimate(flops=flops // 1000, bytes_accessed=size // 1000, transcendentals=0),
    )(*args)


def chunk_rows(chunks, rows, part):
    table = np.zeros((3, chunks, 2, 8, chunks * rows), np.float32)
    for chunk in range(chunks):
        for lane in range(8):
            table[0, chunk, part, lane, chunk * rows + lane] = 1
            table[1, chunk, part, lane, chunk * rows + 8 + lane] = 1
        for lane in range(6):
            table[2, chunk, part, lane, chunk * rows + 16 + lane % 2] = 1
    return table.reshape(3 * chunks * 16, chunks * rows).astype(jnp.bfloat16)


def mix_out(
    x_hbm, attn_hbm, w_space_hbm, recv_hbm, w_time_hbm, mixed_ref,
    x_ref, attn_ref, w_space_ref, time_ref, w_time_ref, sems,
):
    width = x_ref.shape[1]
    loads = load_all(
        [
            (x_hbm, x_ref),
            (attn_hbm, attn_ref),
            (w_space_hbm, w_space_ref),
            (recv_hbm.at[:, pl.ds(width, HK)], time_ref),
            (w_time_hbm, w_time_ref),
        ],
        sems,
    )
    for load in loads:
        load.wait()
    hidden = (x_ref[...].astype(F32) + dot_nn(attn_ref[...], w_space_ref[...])).astype(BF16)
    mixed = hidden.astype(F32) + dot_nn(time_ref[...], w_time_ref[...])
    mixed_ref[...] = mixed.astype(BF16)


def pair_up(core, dqkv, attn, keep_ref, send_ref):
    second = jnp.concatenate([dqkv[:, 2 * HK :], attn], axis=1)
    first = dqkv[:, : 2 * HK]
    keep_ref[...] = jnp.where(core == 0, first, second)
    send_ref[...] = jnp.where(core == 0, second, first)


def weight_terms(lines, in_own, in_got, out_own, out_got, own_ref, got_ref, *refs):
    parts, total_ref = refs[:-1], refs[-1]
    width = own_ref.shape[1]
    low, high = HK // LANES * LANES, -(-HK // LANES) * LANES
    size = width // 3
    rows = width // (lines * lines)
    core = lax.axis_index("c")

    def product(one, two, left, right):
        return dot_tn(one, own_ref[:, left:right]) + dot_tn(two, got_ref[:, left:right])

    def place(me, order):
        for step, part_ref in enumerate(parts):
            line = lax.rem(me + step, lines)
            blocks = []
            for block in range(lines):
                start = pl.multiple_of(order(block, line) * rows, 8)
                blocks.append(total_ref[pl.ds(start, rows), :])
            part_ref[...] = jnp.concatenate(blocks, axis=0).astype(BF16)

    @pl.when(core == 0)
    def _():
        for start in range(0, width, size):
            block = slice(start, start + size)
            total_ref[block, :] = product(in_own[:, block], in_got[:, block], 0, width)
        place(lax.axis_index("z"), lambda block, line: line * lines + block)

    @pl.when(core != 0)
    def _():
        for start in range(0, width, size):
            block = slice(start, start + size)
            left = product(in_own[:, block], in_got[:, block], 0, high)
            right = product(out_own[:, block], out_got[:, block], low, width)
            lane = low + lax.broadcasted_iota(jnp.int32, (size, high - low), 1)
            total_ref[block, :low] = left[:, :low]
            total_ref[block, low:high] = jnp.where(lane < HK, left[:, low:], right[:, : high - low])
            total_ref[block, high:] = right[:, high - low :]
        place(lax.axis_index("y"), lambda block, line: block * lines + line)


def add_lines(table_ref, *refs):
    got, chunk_ref = refs[:4], refs[-1]
    width = got[0].shape[1]
    third = width // 3
    total = got[0][...].astype(F32)
    for ref in got[1:4]:
        total = total + ref[...].astype(F32)
    total = total.astype(BF16)
    block = table_ref.shape[0] // 3
    for part in range(3):
        whole = dot_nn(table_ref[part * block : (part + 1) * block, :], total)
        place = slice(part * width, min((part + 1) * width, 2 * width + third))
        if part == 2:
            row = lax.rem(lax.broadcasted_iota(jnp.int32, (block, third), 0), 8)
            whole = jnp.where(
                row < 2,
                whole[:, :third],
                jnp.where(row < 4, whole[:, third : 2 * third], whole[:, 2 * third :]),
            )
        whole = whole.astype(BF16)
        if len(refs) == 6:
            other = refs[4][:, place]
            row = lax.rem(lax.broadcasted_iota(jnp.int32, whole.shape, 0), 16)
            whole = jnp.where(row < 8, other, whole)
        chunk_ref[:, place] = whole


def add_chunks(scale, chunk_ref, keep_ref, send_ref):
    count, lanes = chunk_ref.shape
    total = chunk_ref[:16, :].astype(F32)
    for start in range(16, count, 16):
        total = total + chunk_ref[start : start + 16, :].astype(F32)
    total = total * scale
    width = lanes // 7 * 3
    third = width // 3
    core = lax.axis_index("c")
    for part in range(2):
        held = total[8 * part : 8 * part + 8]
        first, second, rest = held[:, :width], held[:, width : 2 * width], held[:, 2 * width :]
        last = jnp.concatenate([rest[0:2], rest[2:4], rest[4:6]], axis=1)
        low = jnp.concatenate([first, second[:1]], axis=0)
        high = jnp.concatenate([second[1:], last], axis=0)
        keep_ref[part] = jnp.where(core == 0, low, high)
        send_ref[part] = jnp.where(core == 0, high, low)


def place_rows(keep_ref, got_ref, qkv_time_ref, out_time_ref, qkv_space_ref, out_space_ref):
    core = lax.axis_index("c")
    for part, (qkv_ref, out_ref) in enumerate(
        ((qkv_time_ref, out_time_ref), (qkv_space_ref, out_space_ref))
    ):
        keep, got = keep_ref[part], got_ref[part]
        first = jnp.where(core == 0, keep, got)
        second = jnp.where(core == 0, got, keep)
        qkv_ref[:, : 2 * HK] = first
        qkv_ref[:, 2 * HK :] = second[:, :HK]
        out_ref[...] = second[:, HK:]


SEQ = ("z", "y", "xl")
ALL = ("z", "y", "xl", "xh", "c")
SIDE = 4


def device(z, y, x, core):
    return ((z * SIDE + y) * SIDE + x) * 2 + core


def line_pairs(step):
    pairs = []
    for z in range(SIDE):
        for y in range(SIDE):
            for x in range(SIDE):
                pairs.append((device(z, y, x, 0), device((z + step) % SIDE, y, x, 0)))
                pairs.append((device(z, y, x, 1), device(z, (y + step) % SIDE, x, 1)))
    return pairs


def plane_groups():
    side = range(SIDE)
    groups = [[device(z, y, x, 0) for y in side for x in side] for z in side]
    return groups + [[device(z, y, x, 1) for z in side for x in side] for y in side]


def on_device(clips, cotangent, w_qkv_space, w_out_space, w_qkv_time, w_out_time):
    patches, width = clips.shape[2], clips.shape[3]
    frames = lax.axis_size(SEQ)
    own_patches = patches // frames
    count = patches
    qkv_cols = w_qkv_space.shape[1]
    w_qkv_space, w_out_space = w_qkv_space.T, w_out_space.T
    w_qkv_time, w_out_time = w_qkv_time.T, w_out_time.T
    scale = 1.0 / math.sqrt(count * frames * lax.axis_size(("xh", "c")))
    x = clips.reshape(count, width)
    top = cotangent.reshape(count, width)
    plane = SIDE * SIDE
    rows = width // (plane * SIDE)
    tables = [jnp.asarray(chunk_rows(plane, rows, part)) for part in range(2)]
    half = ((count, width), BF16)
    quarter = ((width // SIDE, width), BF16)

    def swap(array):
        return lax.ppermute(array, "c", [(0, 1), (1, 0)])

    def exchange(array, axes, parts, groups=None):
        lanes = array.shape[1]
        array = lax.all_to_all(
            array.reshape(parts, -1, lanes),
            axes,
            split_axis=0,
            concat_axis=0,
            tiled=True,
            axis_index_groups=groups,
        )
        return array.reshape(-1, lanes)

    def terms(*args):
        return call(
            functools.partial(weight_terms, SIDE),
            [quarter] * SIDE,
            *args,
            flops=2 * 10**9,
            scratch=[pltpu.VMEM((width, width), F32)],
            grant=16,
        )

    def along_lines(parts):
        return [parts[0]] + [
            lax.ppermute(part, ALL, line_pairs(step)) for step, part in enumerate(parts) if step
        ]

    def buffers(*shapes):
        return [pltpu.VMEM(*shape) for shape in shapes]

    qkv = ((count, qkv_cols), BF16)
    mix = ((count, HK), BF16)
    send, qkv_space, attn_space, normed_space = call(
        space_forward,
        [((count, 2 * width), BF16), qkv, mix, half],
        x, top, w_qkv_space, w_out_space,
        flops=3 * 10**9,
        hbm_in=4,
        hbm_out=(1, 2, 3),
        scratch=buffers(half, ((qkv_cols, width), BF16), ((HK, width), BF16), qkv, mix, half)
        + [pltpu.SemaphoreType.DMA((9,))],
        grant=16,
    )
    recv = exchange(send, SEQ, frames)
    pack = ((count, width + HK), BF16)
    back, normed_time, top_time, keep, give = call(
        functools.partial(time_both, own_patches),
        [pack, half, half, half, half],
        recv, w_qkv_time, w_out_time,
        flops=5 * 10**9,
        hbm_out=(0, 1, 2, 3, 4),
        scratch=buffers(pack, half, half, half) + [pltpu.SemaphoreType.DMA((6,))],
        grant=16,
    )
    terms_time = terms(
        normed_time, swap(normed_time), top_time, swap(top_time), keep, swap(give)
    )
    recv = exchange(back, SEQ, frames)
    recv, terms_time = lax.optimization_barrier((recv, terms_time))
    got_time = along_lines(terms_time)
    wide = ((HK, width), BF16)
    dhidden, dqkv_space, keep, give, normed_space = call(
        space_backward, [half, qkv, half, half, half],
        top, recv, w_out_space, qkv_space, attn_space, normed_space,
        flops=3 * 10**9,
        hbm_in=6,
        scratch=buffers(half, half, wide, qkv, mix) + [pltpu.SemaphoreType.DMA((6,))],
        grant=20,
    )
    keep, got_time[1], got_time[3] = lax.optimization_barrier((keep, got_time[1], got_time[3]))
    terms_space = terms(
        normed_space, swap(normed_space), dhidden, swap(dhidden), keep, swap(give)
    )
    got_space = along_lines(terms_space)
    grad_clips = call(
        space_finish, [half], x, w_qkv_space, dhidden, dqkv_space,
        flops=10**9,
        hbm_in=2,
        scratch=buffers(half, ((qkv_cols, width), BF16)) + [pltpu.SemaphoreType.DMA((2,))],
        grant=16,
    )[0]
    mixed = call(
        mix_out, [half], x, attn_space, w_out_space, recv, w_out_time,
        flops=10**9,
        hbm_in=5,
        scratch=buffers(half, mix, wide, mix, wide) + [pltpu.SemaphoreType.DMA((5,))],
        grant=16,
    )[0]
    chunk = [((plane * 16, 2 * width + width // 3), BF16)]
    chunks = call(add_lines, chunk, tables[0], *got_time, flops=10**9)[0]
    chunks = call(add_lines, chunk, tables[1], *got_space, chunks, flops=10**9)[0]
    chunks, grad_clips, mixed = lax.optimization_barrier((chunks, grad_clips, mixed))
    chunks = exchange(chunks, ALL, plane, plane_groups())
    own_rows = ((2, rows // 2, width), F32)
    own, other = call(functools.partial(add_chunks, scale), [own_rows, own_rows], chunks)
    grad_qkv = ((rows // 2, qkv_cols), F32)
    grad_out = ((rows // 2, HK), F32)
    grad_qkv_time, grad_out_time, grad_qkv_space, grad_out_space = call(
        place_rows, [grad_qkv, grad_out, grad_qkv, grad_out], own, swap(other)
    )
    return (
        mixed.reshape(clips.shape),
        grad_clips.reshape(clips.shape),
        grad_qkv_space,
        grad_out_space,
        grad_qkv_time,
        grad_out_time,
    )


def solution(mesh):
    fine = Mesh(mesh.devices.reshape(4, 4, 2, 2, 2), ("z", "y", "xl", "xh", "c"))
    tokens = P(("xh", "c"), SEQ, None, None)
    rows = P(("z", "y", "xl", "xh", "c"), None)
    return jax.shard_map(
        on_device,
        mesh=fine,
        in_specs=(tokens, tokens, P(), P(), P(), P()),
        out_specs=(tokens, tokens, rows, rows, rows, rows),
        check_vma=False,
    )
```
